256 devices in a mesh: lon: 32 (over z, y_hi, core), lat: 8 (over y_lo, x).
Axes of the slice: x: 4, y: 4 (y_hi: 2, y_lo: 2; y = y_hi * 2 + y_lo), z: 8, core: 2. Of those that a mesh axis runs over, the one named last changes fastest.
Arguments:
- zonal_flow: float32 [4, 1024, 4096], P(None, 'lat', 'lon'), as said below
- meridional_flow: float32 [4, 1024, 4096], P(None, 'lat', 'lon'), as said below
- tracers: float32 [3, 4, 1024, 4096], P(None, None, 'lat', 'lon'), may hold values from -6 to 6
- sea_mask: int32 [4, 1024, 4096], P(None, 'lat', 'lon'), may hold values from 0 to 1, as said below
- diffusivity: float32 [3, 1024, 4096], P(None, 'lat', 'lon'), may hold values from 0.05 to 5
Outputs:
- zonal_out: float32 [4, 1024, 4096], P(None, 'lat', 'lon')
- meridional_out: float32 [4, 1024, 4096], P(None, 'lat', 'lon')
- tracers_out: float32 [3, 4, 1024, 4096], P(None, None, 'lat', 'lon')
The draws below stay inside these ranges and needn't reach their ends.
Inputs may be any that keep to these rules, and one draw needn't show every extreme that they name: There is a stream function s of shape [4, 1024, 4096] on cell corners with |s| <= 0.12, zero below row 0 and periodic in longitude, such that zonal_flow[k, j, i] = s[k, j - 1, i] - s[k, j, i]; the discrete divergence of the two velocities vanishes. meridional_flow[k, j, i] = s[k, j, i] - s[k, j, i - 1] with the same stream function s as zonal_flow. `sea_mask`: A cell is sea only where the cell above it, at level k - 1, is sea.
All inputs are finite; a program needn't handle non-finite values.
Results may differ from the reference program's by a relative error of at most 0.0003.
Values sent between devices are 32-bit elements; how exact they have to be, the bound alone decides.
A program may use at most 64 MiB of HBM per device.

```python
import math
import jax
import jax.numpy as jnp
from jax import lax

K = 4
TRACERS = 3
NSUB = 3
NX = 4096
NY = 1024


def stream_function(key, spread):
    raw_values = spread * jax.random.normal(key, (K, NY, NX), jnp.float32)
    return jnp.clip(raw_values, -0.12, 0.12)


def draw_zonal_flow(key, part):
    spread = 0.05
    stream = stream_function(key, spread)
    southern = jnp.concatenate([jnp.zeros((K, 1, NX), jnp.float32), stream[:, :-1, :]], axis=1)
    return southern - stream


def draw_meridional_flow(key, part):
    spread = 0.05
    stream = stream_function(key, spread)
    return stream - jnp.roll(stream, 1, axis=2)


def draw_sea_mask(key, part):
    key = jax.random.fold_in(key, 11)
    column_depth = jnp.minimum(jax.random.randint(key, (NY, NX), 0, K + 3), K)
    stratum = lax.broadcasted_iota(jnp.int32, (K, NY, NX), 0)
    return (stratum < column_depth[None]).astype(jnp.int32)


def shard_levels(own_key, dims, split, smallest, high):
    def one(axis_at, parts):
        draws = jax.random.uniform(jax.random.fold_in(jax.random.fold_in(own_key, 6), axis_at), (parts,), jnp.float32, smallest / len(split), high / len(split))
        return jnp.repeat(jnp.exp(draws), dims[axis_at] // parts).reshape((-1,) + (1,) * (len(dims) - axis_at - 1))

    factor_of = one(*split[0])
    for cut in split[1:]:
        factor_of = factor_of * one(*cut)
    return factor_of


def noise(own_key, shape, scale, limit, shards=(), held_as=jnp.bfloat16):
    drawn = scale * jax.random.normal(own_key, shape, jnp.float32)
    if shards:
        drawn = drawn * shard_levels(own_key, shape, shards, -0.22, 0.18)
    return jnp.clip(drawn, -limit, limit).astype(held_as)


def setup_inputs(seed: int = 0) -> dict:
    streams_of = jax.random.split(jax.random.key(seed), 6)
    zonal_flow = draw_zonal_flow(jax.random.fold_in(streams_of[5], 71), 0)
    meridional_flow = draw_meridional_flow(jax.random.fold_in(streams_of[5], 71), 0)
    tracers = noise(streams_of[2], (TRACERS, K, NY, NX), 1.0, 6.0, ((2, 8), (3, 32)), jnp.float32)
    sea_mask = draw_sea_mask(jax.random.fold_in(streams_of[5], 71), 0)
    diffusivity = jnp.clip(jnp.exp(math.log(5.0) - 4.6051702 * jax.random.uniform(streams_of[4], (K - 1, NY, NX), jnp.float32) ** shard_levels(streams_of[4], (K - 1, NY, NX), ((1, 8), (2, 32)), -0.2, 0.2)), 0.05, 5.0)
    return {"zonal_flow": zonal_flow, "meridional_flow": meridional_flow, "tracers": tracers, "sea_mask": sea_mask, "diffusivity": diffusivity}


coriolis_peak = 0.5


def extend(field, signs):
    height = field.shape[2]
    southern = jnp.zeros(field.shape[:2] + (2, field.shape[3]), field.dtype)
    flipped = jnp.flip(field[:, :, height - 2:, :], axis=(2, 3))
    northern = flipped * jnp.asarray(signs, field.dtype)[:, None, None, None]
    tall_field = jnp.concatenate([southern, field, northern], axis=2)
    return jnp.concatenate([tall_field[..., -2:], tall_field, tall_field[..., :2]], axis=3)


def minmod(forward, backward):
    return 0.5 * (jnp.sign(forward) + jnp.sign(backward)) * jnp.minimum(jnp.abs(forward), jnp.abs(backward))


def section(array, begin_at, end_at, axis_num):
    return lax.slice_in_dim(array, begin_at, end_at, axis=axis_num)


def divergence(values_ext, wet_ext, velocity_ext, axis_num):
    extent = values_ext.shape[axis_num]
    open_faces = section(wet_ext, 1, extent, axis_num) * section(wet_ext, 0, extent - 1, axis_num)
    increments = (section(values_ext, 1, extent, axis_num) - section(values_ext, 0, extent - 1, axis_num)) * open_faces
    slopes = minmod(section(increments, 1, extent - 1, axis_num), section(increments, 0, extent - 2, axis_num))
    upwind = section(values_ext, 1, extent - 2, axis_num)
    downwind = section(values_ext, 2, extent - 1, axis_num)
    slope_left = section(slopes, 0, extent - 3, axis_num)
    slope_right = section(slopes, 1, extent - 2, axis_num)
    velocity = section(velocity_ext, 1, extent - 2, axis_num)
    face_gate = section(open_faces, 1, extent - 2, axis_num)
    fluxes = face_gate * (jnp.maximum(velocity, 0.0) * (upwind + 0.5 * (1.0 - velocity) * slope_left)
                          + jnp.minimum(velocity, 0.0) * (downwind - 0.5 * (1.0 + velocity) * slope_right))
    face_count = extent - 3
    return section(fluxes, 1, face_count, axis_num) - section(fluxes, 0, face_count - 1, axis_num)


def momentum(zonal_ext, meridional_ext, wet_ext, coriolis_u, coriolis_v):
    zonal_here = zonal_ext[:, 2:-2, 2:-2]
    zonal_east = zonal_ext[:, 2:-2, 3:-1]
    zonal_west = zonal_ext[:, 2:-2, 1:-3]
    zonal_north = zonal_ext[:, 3:-1, 2:-2]
    zonal_south = zonal_ext[:, 1:-3, 2:-2]
    zonal_northwest = zonal_ext[:, 3:-1, 1:-3]
    meridional_here = meridional_ext[:, 2:-2, 2:-2]
    meridional_east = meridional_ext[:, 2:-2, 3:-1]
    meridional_west = meridional_ext[:, 2:-2, 1:-3]
    meridional_north = meridional_ext[:, 3:-1, 2:-2]
    meridional_south = meridional_ext[:, 1:-3, 2:-2]
    meridional_southeast = meridional_ext[:, 1:-3, 3:-1]
    wet_here = wet_ext[:, 2:-2, 2:-2]
    wet_east = wet_ext[:, 2:-2, 3:-1]
    wet_north = wet_ext[:, 3:-1, 2:-2]
    cross_meridional = 0.25 * (meridional_here + meridional_east + meridional_south + meridional_southeast)
    cross_zonal = 0.25 * (zonal_here + zonal_north + zonal_west + zonal_northwest)
    zonal_change = (-zonal_here * (zonal_east - zonal_west) * 0.5
                    - cross_meridional * (zonal_north - zonal_south) * 0.5
                    + coriolis_u * cross_meridional)
    meridional_change = (-cross_zonal * (meridional_east - meridional_west) * 0.5
                         - meridional_here * (meridional_north - meridional_south) * 0.5
                         - coriolis_v * cross_zonal)
    zonal_gate = wet_here * wet_east
    meridional_gate = wet_here * wet_north
    zonal_new = zonal_here + zonal_gate * zonal_change
    meridional_new = meridional_here + meridional_gate * meridional_change
    return zonal_new, meridional_new, zonal_gate, meridional_gate


def mix_columns(field, coupling):
    levels = field.shape[1]
    nothing = jnp.zeros_like(coupling[:, 0])
    ratios = []
    scaled = []
    for stratum in range(levels):
        lower_coef = coupling[:, stratum - 1] if stratum > 0 else nothing
        upper_coef = coupling[:, stratum] if stratum < levels - 1 else nothing
        divisor = 1.0 + lower_coef + upper_coef
        source = field[:, stratum]
        if stratum > 0:
            divisor = divisor + lower_coef * ratios[-1]
            source = source + lower_coef * scaled[-1]
        ratios.append(-upper_coef / divisor)
        scaled.append(source / divisor)
    solved = [scaled[-1]]
    for stratum in range(levels - 2, -1, -1):
        solved.insert(0, scaled[stratum] - ratios[stratum] * solved[0])
    return jnp.stack(solved, axis=1)


def reference(zonal_flow, meridional_flow, tracers, sea_mask, diffusivity):
    wet_cells = sea_mask.astype(jnp.float32)
    latitude = jnp.arange(NY).astype(jnp.float32)
    coriolis_u = (coriolis_peak * jnp.sin(math.pi * ((latitude + 0.5) / NY - 0.5)))[:, None]
    coriolis_v = (coriolis_peak * jnp.sin(math.pi * ((latitude + 1.0) / NY - 0.5)))[:, None]

    def horizontal(inputs):
        zonal_level, meridional_level, tracer_level, wet_level = inputs
        flows_ext = extend(jnp.stack([zonal_level, meridional_level])[:, None], [-1.0, -1.0])
        wet_ext = extend(wet_level[None, None], [1.0])[0]
        zonal_ext = flows_ext[0]
        meridional_ext = flows_ext[1]
        zonal_new, meridional_new, zonal_gate, meridional_gate = momentum(
            zonal_ext, meridional_ext, wet_ext, coriolis_u, coriolis_v)
        wet_x = wet_ext[None, :, 2:-2, :]
        wet_y = wet_ext[None, :, :, 2:-2]
        zonal_x = zonal_ext[None, :, 2:-2, :]
        meridional_y = meridional_ext[None, :, :, 2:-2]
        tracer_now = tracer_level[:, None]
        for substep in range(NSUB):
            grown = extend(tracer_now, [1.0] * TRACERS)
            tracer_now = (tracer_now
                          - divergence(grown[:, :, 2:-2, :], wet_x, zonal_x, 3)
                          - divergence(grown[:, :, :, 2:-2], wet_y, meridional_y, 2))
        return zonal_new[0], meridional_new[0], zonal_gate[0], meridional_gate[0], tracer_now[:, 0]

    zonal_new, meridional_new, zonal_gate, meridional_gate, tracer_after = lax.map(
        horizontal, (zonal_flow, meridional_flow, jnp.moveaxis(tracers, 1, 0), wet_cells))
    tracer_after = jnp.moveaxis(tracer_after, 0, 1)
    wet_pairs = wet_cells[:-1] * wet_cells[1:]
    tracer_coupling = (diffusivity * wet_pairs)[None]
    mixed = []
    for tracer_index in range(TRACERS):
        mixed.append(mix_columns(tracer_after[tracer_index:tracer_index + 1], tracer_coupling))
    tracers_out = jnp.concatenate(mixed, axis=0)
    zonal_out = mix_columns(zonal_new[None], (diffusivity * zonal_gate[:-1] * zonal_gate[1:])[None])[0]
    meridional_out = mix_columns(meridional_new[None], (diffusivity * meridional_gate[:-1] * meridional_gate[1:])[None])[0]
    return zonal_out, meridional_out, tracers_out
```

```python
import functools
import math

import jax
import jax.numpy as jnp
from jax import lax
from jax.experimental import pallas as pl
from jax.experimental.pallas import tpu as pltpu
from jax.sharding import PartitionSpec as P

K = 4
T = 3
NSUB = 3
B = 128
H = 8
E = B + 2 * H
R = E // 8
F32 = jnp.float32
MESH = pl.DeviceIdType.MESH
coriolis_peak = 0.5


def exchange(nlat, nlon, u, v, q, m, rn, rs, mn, ms, pe, pw, xv, mv, ke, kw, load, send, recv):
    lat = lax.axis_index("lat")
    lon = lax.axis_index("lon")
    top = lat == nlat - 1
    bottom = lat == 0
    east = lax.rem(lon + 1, nlon)
    west = lax.rem(lon + nlon - 1, nlon)
    n_lat = jnp.where(top, lat, lat + 1)
    n_mid = jnp.where(top, nlon - 1 - lon, lon)
    n_west = jnp.where(top, lax.rem(nlon - lon, nlon), west)
    n_east = jnp.where(top, lax.rem(2 * nlon - 2 - lon, nlon), east)
    s_lat = jnp.maximum(lat - 1, 0)
    own_w = n_west == lon
    own_e = n_east == lon

    def at(row, column):
        return {"lat": row, "lon": column}

    loads = [
        pltpu.make_async_copy(u, xv.at[0:K], load.at[0]),
        pltpu.make_async_copy(v, xv.at[K : 2 * K], load.at[1]),
        pltpu.make_async_copy(q, xv.at[2 * K :], load.at[2]),
        pltpu.make_async_copy(m, mv, load.at[3]),
    ]
    for copy in loads:
        copy.start()

    barrier = pltpu.get_barrier_semaphore()

    def greet(row, column):
        pl.semaphore_signal(barrier, inc=1, device_id=at(row, column), device_id_type=MESH)

    greet(lat, east)
    greet(lat, west)
    greet(n_lat, n_mid)

    @pl.when(jnp.logical_not(top & own_w))
    def _():
        greet(n_lat, n_west)

    @pl.when(jnp.logical_not(top & own_e))
    def _():
        greet(n_lat, n_east)

    @pl.when(jnp.logical_not(bottom))
    def _():
        greet(s_lat, lon)
        greet(s_lat, west)
        greet(s_lat, east)

    peers = (
        3
        + jnp.where(top & own_w, 0, 1)
        + jnp.where(top & own_e, 0, 1)
        + jnp.where(bottom, 0, 3)
    )
    pl.semaphore_wait(barrier, peers)

    def remote(src, dst, slot, row, column):
        return pltpu.make_async_remote_copy(
            src_ref=src,
            dst_ref=dst,
            send_sem=send.at[slot],
            recv_sem=recv.at[slot],
            device_id=at(row, column),
            device_id_type=MESH,
        )

    hi = pl.ds(B - H, H)
    lo = pl.ds(0, H)

    def rows(part, fields, marks, base, row, column):
        return [
            remote(u.at[:, part], fields.at[0:K], base, row, column),
            remote(v.at[:, part], fields.at[K : 2 * K], base + 1, row, column),
            remote(q.at[:, part], fields.at[2 * K :], base + 2, row, column),
            remote(m.at[:, part], marks, base + 3, row, column),
        ]

    to_north = rows(hi, rs, ms, 8, n_lat, n_mid)
    over_fold = rows(hi, rn, mn, 2, n_lat, n_mid)
    to_south = rows(lo, rn, mn, 2, s_lat, lon)

    @pl.when(top)
    def _():
        for copy in over_fold:
            copy.start()

    @pl.when(jnp.logical_not(top))
    def _():
        for copy in to_north:
            copy.start()

    @pl.when(jnp.logical_not(bottom))
    def _():
        for copy in to_south:
            copy.start()

    for copy in loads:
        copy.wait()

    group = lax.broadcasted_iota(jnp.int32, (8, B), 1) // 8

    def pack(i, carry):
        part = pl.ds(pl.multiple_of(i * 8, 8), 8)
        for half in range(2):
            packed_w = jnp.zeros((8, B), F32)
            packed_e = jnp.zeros((8, B), F32)
            for k in range(K):
                for f in range(4 if half == 0 else 2):
                    if half == 1:
                        x = xv[f * K + k, part]
                    elif f < T:
                        x = xv[2 * K + f * K + k, part]
                    else:
                        x = mv[k, part].astype(F32)
                    j = 4 * k + f
                    x = pltpu.roll(x, 8 * j, 1) if j else x
                    packed_w = jnp.where(group == j, x, packed_w)
                    packed_e = jnp.where(group == (j - 1) % 16, x, packed_e)
            kw[half, part] = packed_w
            ke[half, part] = packed_e
        return carry

    lax.fori_loop(0, B // 8, pack, 0)

    middle = pl.ds(H, B)
    beyond = pl.ds(H + B, H)
    sends = [
        remote(ke, pw.at[:, middle], 1, lat, east),
        remote(kw, pe.at[:, middle], 0, lat, west),
    ]
    for copy in sends:
        copy.start()
    north_east = remote(ke.at[:, hi], pw.at[:, lo], 13, n_lat, n_east)
    north_west = remote(kw.at[:, hi], pe.at[:, lo], 12, n_lat, n_west)
    fold_west = remote(kw.at[:, hi], pw.at[:, beyond], 7, n_lat, n_west)
    fold_east = remote(ke.at[:, hi], pe.at[:, beyond], 6, n_lat, n_east)
    self_west = pltpu.make_async_copy(kw.at[:, hi], pw.at[:, beyond], load.at[4])
    self_east = pltpu.make_async_copy(ke.at[:, hi], pe.at[:, beyond], load.at[5])
    south_east = remote(ke.at[:, lo], pw.at[:, beyond], 7, s_lat, east)
    south_west = remote(kw.at[:, lo], pe.at[:, beyond], 6, s_lat, west)

    @pl.when(jnp.logical_not(top))
    def _():
        north_east.start()
        north_west.start()

    @pl.when(top & own_w)
    def _():
        self_west.start()

    @pl.when(top & jnp.logical_not(own_w))
    def _():
        fold_west.start()

    @pl.when(top & own_e)
    def _():
        self_east.start()

    @pl.when(top & jnp.logical_not(own_e))
    def _():
        fold_east.start()

    @pl.when(jnp.logical_not(bottom))
    def _():
        south_east.start()
        south_west.start()

    for copy in sends:
        copy.wait_send()

    @pl.when(top)
    def _():
        for copy in over_fold:
            copy.wait_send()

    @pl.when(jnp.logical_not(top))
    def _():
        for copy in to_north:
            copy.wait_send()
        north_east.wait_send()
        north_west.wait_send()

    @pl.when(top & own_w)
    def _():
        self_west.wait()

    @pl.when(top & jnp.logical_not(own_w))
    def _():
        fold_west.wait_send()

    @pl.when(top & own_e)
    def _():
        self_east.wait()

    @pl.when(top & jnp.logical_not(own_e))
    def _():
        fold_east.wait_send()

    @pl.when(jnp.logical_not(bottom))
    def _():
        for copy in to_south:
            copy.wait_send()
        south_east.wait_send()
        south_west.wait_send()

    for copy in sends:
        copy.wait_recv()
    for copy in to_south:
        copy.wait_recv()

    @pl.when(jnp.logical_not(top & own_w))
    def _():
        south_east.wait_recv()

    @pl.when(jnp.logical_not(top & own_e))
    def _():
        south_west.wait_recv()

    @pl.when(jnp.logical_not(bottom))
    def _():
        for copy in to_north:
            copy.wait_recv()
        north_east.wait_recv()
        north_west.wait_recv()


def exchanged(nlat, nlon, u, v, q, m):
    any_space = pl.BlockSpec(memory_space=pl.ANY)
    return pl.pallas_call(
        functools.partial(exchange, nlat, nlon),
        out_shape=(
            jax.ShapeDtypeStruct(((2 + T) * K, H, B), F32),
            jax.ShapeDtypeStruct(((2 + T) * K, H, B), F32),
            jax.ShapeDtypeStruct((K, H, B), jnp.int32),
            jax.ShapeDtypeStruct((K, H, B), jnp.int32),
            jax.ShapeDtypeStruct((2, E, B), F32),
            jax.ShapeDtypeStruct((2, E, B), F32),
        ),
        in_specs=[any_space] * 4,
        out_specs=[any_space] * 6,
        scratch_shapes=[
            pltpu.VMEM(((2 + T) * K, B, B), F32),
            pltpu.VMEM((K, B, B), jnp.int32),
            pltpu.VMEM((2, B, B), F32),
            pltpu.VMEM((2, B, B), F32),
            pltpu.SemaphoreType.DMA((6,)),
            pltpu.SemaphoreType.DMA((14,)),
            pltpu.SemaphoreType.DMA((14,)),
        ],
        compiler_params=pltpu.CompilerParams(
            collective_id=0, has_side_effects=True, vmem_limit_bytes=32 * 2**20
        ),
    )(u, v, q, m)


def minmod(a, b):
    return jnp.maximum(jnp.minimum(a, b), jnp.minimum(jnp.maximum(a, b), 0.0))


def following(x):
    return pltpu.roll(x, B - 1, 1)


def preceding(x):
    return pltpu.roll(x, 1, 1)


def above(x):
    return pltpu.roll(x, 7, 0)


def below(x):
    return pltpu.roll(x, 1, 0)


def rolled(x, amount):
    return pltpu.roll(x, amount % B, 1) if amount % B else x


def flipped(x, index):
    x = jnp.take_along_axis(x, index, axis=1)
    backward = 7 - lax.broadcasted_iota(jnp.int32, (8, B), 0)
    return jnp.take_along_axis(x, backward, axis=0)


def solve(x, coupling):
    carried = []
    inverse = []
    for k in range(K):
        divisor = 1.0
        if k < K - 1:
            divisor = divisor + coupling[k]
        if k > 0:
            divisor = divisor + coupling[k - 1] * (1.0 - carried[k - 1])
        inverse.append(1.0 / divisor)
        if k < K - 1:
            carried.append(coupling[k] * inverse[k])
    results = []
    for field in x:
        scaled = [field[0] * inverse[0]]
        for k in range(1, K):
            scaled.append((field[k] + coupling[k - 1] * scaled[k - 1]) * inverse[k])
        solved = [scaled[K - 1]]
        for k in range(K - 2, -1, -1):
            solved.insert(0, scaled[k] + carried[k] * solved[0])
        results.append(solved)
    return results


def compute(
    nlat, u, v, q, m, d, rn, rs, mn, ms, pe, pw, uo, vo, qo,
    ext, mext, dext, pks, flow, new, tr, wet, cx, cy, fold, load, store,
):
    lat = lax.axis_index("lat")
    top = lat == nlat - 1
    bottom = lat == 0
    middle = pl.ds(H, B)
    lo = pl.ds(0, H)
    beyond = pl.ds(H + B, H)
    N = (2 + T) * K
    copies = [
        pltpu.make_async_copy(u, ext.at[0:K, middle], load.at[0]),
        pltpu.make_async_copy(v, ext.at[K : 2 * K, middle], load.at[1]),
        pltpu.make_async_copy(q, ext.at[2 * K :, middle], load.at[2]),
        pltpu.make_async_copy(m, mext.at[:, middle], load.at[3]),
        pltpu.make_async_copy(rn, ext.at[:, beyond], load.at[4]),
        pltpu.make_async_copy(rs, ext.at[:, lo], load.at[5]),
        pltpu.make_async_copy(mn, mext.at[:, beyond], load.at[6]),
        pltpu.make_async_copy(ms, mext.at[:, lo], load.at[7]),
        pltpu.make_async_copy(pe, pks.at[0], load.at[8]),
        pltpu.make_async_copy(pw, pks.at[1], load.at[9]),
        pltpu.make_async_copy(d, dext.at[:, middle], load.at[10]),
    ]
    for copy in copies:
        copy.start()
    for copy in copies[:-1]:
        copy.wait()

    lane = lax.broadcasted_iota(jnp.int32, (8, B), 1)
    sub = lax.broadcasted_iota(jnp.int32, (8, B), 0)

    @pl.when(bottom)
    def _():
        ext[:, lo] = jnp.zeros((N, H, B), F32)
        mext[:, lo] = jnp.zeros((K, H, B), jnp.int32)
        pks[:, :, lo] = jnp.zeros((2, 2, H, B), F32)

    @pl.when(top)
    def _():
        whole = B - 1 - lane
        for f in range(N):
            x = flipped(ext[f, beyond], whole)
            ext[f, beyond] = -x if f < 2 * K else x
        for k in range(K):
            mext[k, beyond] = flipped(mext[k, beyond].astype(F32), whole).astype(jnp.int32)
        within = 7 - lane % 8
        from_east = (lane // 8 + 15) % 16 * 8 + within
        from_west = (lane // 8 + 1) % 16 * 8 + within
        for half in range(2):
            x = flipped(pks[0, half, beyond], from_east)
            pks[0, half, beyond] = -x if half else x
            x = flipped(pks[1, half, beyond], from_west)
            pks[1, half, beyond] = -x if half else x

    place = lane % 32
    level = lane // 32
    own_hi = place < 10
    own_lo = place >= 22
    far_hi = (place >= 10) & (place < 16)
    far_lo = (place >= 16) & (place < 22)
    is_hi = [own_hi & (level == k) for k in range(K)]
    is_lo = [own_lo & (level == k) for k in range(K)]

    for r in range(R):
        strided = pl.ds(r, 8, stride=R)
        packs = [[pks[side, half, strided] for half in range(2)] for side in range(2)]
        for f in range(2 + T + 1):
            edge = jnp.zeros((8, B), F32)
            for k in range(K):
                if f < 2 + T:
                    x = ext[f * K + k, strided]
                else:
                    x = mext[k, strided].astype(F32)
                if f < 2:
                    flow[f, k, r] = x
                elif f < 2 + T:
                    tr[f - 2, k, r] = x
                else:
                    wet[k, r] = x
                edge = jnp.where(is_hi[k], rolled(x, 32 * k + 10), edge)
                edge = jnp.where(is_lo[k], rolled(x, 32 * k + 22), edge)
            half, slot = (1, f) if f < 2 else (0, f - 2)
            edge = jnp.where(far_hi, rolled(packs[0][half], 10 - 8 * slot), edge)
            edge = jnp.where(far_lo, rolled(packs[1][half], 22 - 8 * slot), edge)
            if f < 2:
                flow[f, K, r] = edge
            elif f < 2 + T:
                tr[f - 2, K, r] = edge
            else:
                wet[K, r] = edge

    def coriolis(offset):
        row = lat * B + R * sub + lane - H
        ny = nlat * B
        return coriolis_peak * jnp.sin(math.pi * ((row.astype(F32) + offset) / ny - 0.5))

    cor_u = coriolis(0.5)
    cor_v = coriolis(1.0)
    last = top & (sub == 7)

    def prepare(i, carry):
        def get(f, r):
            if r == -1:
                return below(flow[f, i, R - 1])
            if r == R:
                return above(flow[f, i, 0])
            return flow[f, i, r]

        us, vs = get(0, -1), get(1, -1)
        u0, v0 = get(0, 0), get(1, 0)
        w0 = wet[i, 0]
        for r in range(R):
            un, vn = get(0, r + 1), get(1, r + 1)
            wn = wet[i, r + 1] if r < R - 1 else above(wet[i, 0])
            gu = w0 * following(w0)
            gv = w0 * wn
            ue = following(u0)
            ua = jnp.where(last, ue, u0) if r >= R - H else u0
            va = jnp.where(last, vn, v0) if r >= R - H else v0
            cx[0, i, r] = gu
            cx[1, i, r] = ua * gu
            cx[2, i, r] = jnp.where(ua > 0.0, 0.5, -0.5) - 0.5 * ua
            cy[0, i, r] = gv
            cy[1, i, r] = va * gv
            cy[2, i, r] = jnp.where(va > 0.0, 0.5, -0.5) - 0.5 * va
            if r == R - H - 1:
                vf = jnp.where(last, vn, v0)
                fold[0, i] = vf * gv
                fold[1, i] = jnp.where(vf > 0.0, 0.5, -0.5) - 0.5 * vf
            a = v0 + vs
            vbar = 0.25 * (a + following(a))
            a = u0 + un
            ubar = 0.25 * (a + preceding(a))
            fu = jnp.broadcast_to(cor_u[:, r : r + 1], (8, B))
            fv = jnp.broadcast_to(cor_v[:, r : r + 1], (8, B))
            du = vbar * (fu - 0.5 * (un - us)) - 0.5 * u0 * (ue - preceding(u0))
            dv = -ubar * (fv + 0.5 * (following(v0) - preceding(v0))) - 0.5 * v0 * (vn - vs)
            new[0, i, r] = u0 + gu * du
            new[1, i, r] = v0 + gv * dv
            us, vs, u0, v0, w0 = u0, v0, un, vn, wn
        return carry

    lax.fori_loop(0, K + 1, prepare, 0)

    def merged(x, edge, k, low, high):
        if low:
            x = jnp.where(lane < low, rolled(edge, -(32 * k + 22)), x)
        return jnp.where(lane >= high, rolled(edge, 118 - 32 * k), x)

    def face(w, c, here, there, slope_here, slope_there):
        way = w > 0.0
        return w * (jnp.where(way, here, there) + c * jnp.where(way, slope_here, slope_there))

    def advect(i, carry):
        first, turned, last_jump, last_slope = [], [], [], []
        now, ahead, jump, slope, south = [], [], [], [], []
        for t in range(T):
            x0, x1 = tr[t, i, 0], tr[t, i, 1]
            xr = above(x0)
            jr = (xr - tr[t, i, R - 1]) * cy[0, i, R - 1]
            j0 = (x1 - x0) * cy[0, i, 0]
            s0 = minmod(j0, below(jr))
            turned.append(xr)
            last_jump.append(jr)
            last_slope.append(above(s0))
            now.append(x0)
            ahead.append(x1)
            jump.append(j0)
            slope.append(s0)
            south.append(None)
            first.append(None)
        for r in range(R):
            gx, wx, ex = cx[0, i, r], cx[1, i, r], cx[2, i, r]
            wy, ey = cy[1, i, r], cy[2, i, r]
            gy = cy[0, i, r + 1] if r + 1 < R - 1 else None
            for t in range(T):
                x, xn = now[t], ahead[t]
                if r + 1 < R - 1:
                    xnn = tr[t, i, r + 2]
                    jn = (xnn - xn) * gy
                    sn = minmod(jn, jump[t])
                elif r + 1 == R - 1:
                    xnn = turned[t]
                    jn = last_jump[t]
                    sn = minmod(jn, jump[t])
                else:
                    xnn = jn = None
                    sn = last_slope[t]
                north = face(wy, ey, x, xn, slope[t], sn)
                e = following(x)
                j = (e - x) * gx
                s = minmod(j, preceding(j))
                f = face(wx, ex, x, e, s, following(s))
                out = x - (f - preceding(f))
                if r == 0:
                    first[t] = out - north
                else:
                    tr[t, i, r] = out - (north - south[t])
                if r == R - H - 1:
                    north = face(fold[0, i], fold[1, i], x, xn, slope[t], sn)
                south[t] = north
                now[t], ahead[t], jump[t], slope[t] = xn, xnn, jn, sn
        for t in range(T):
            tr[t, i, 0] = first[t] + below(south[t])
        return carry

    copies[-1].wait()
    for r in range(R):
        strided = pl.ds(r, 8, stride=R)
        mix = [dext[k, strided] for k in range(K - 1)]
        gu = [merged(cx[0, k, r], cx[0, K, r], k, 0, B - 1) for k in range(K)]
        gv = [cy[0, k, r] for k in range(K)]
        un = [merged(new[0, k, r], new[0, K, r], k, 1, B - 1) for k in range(K)]
        vn = [merged(new[1, k, r], new[1, K, r], k, 1, B - 1) for k in range(K)]
        (un,) = solve([un], [mix[k] * (gu[k] * gu[k + 1]) for k in range(K - 1)])
        (vn,) = solve([vn], [mix[k] * (gv[k] * gv[k + 1]) for k in range(K - 1)])
        for k in range(K):
            ext[k, strided] = un[k]
            ext[K + k, strided] = vn[k]
    out_u = pltpu.make_async_copy(ext.at[0:K, middle], uo, store.at[0])
    out_v = pltpu.make_async_copy(ext.at[K : 2 * K, middle], vo, store.at[1])
    out_q = pltpu.make_async_copy(ext.at[2 * K :, middle], qo, store.at[2])
    out_u.start()
    out_v.start()

    for step in range(NSUB):
        lax.fori_loop(0, K + 1, advect, 0)
        if step == 0:
            for r in range(R):
                for t in range(T):
                    for k in range(K):
                        tr[t, k, r] = merged(tr[t, k, r], tr[t, K, r], k, 2, B - 2)

    for r in range(R):
        strided = pl.ds(r, 8, stride=R)
        w = [wet[k, r] for k in range(K)]
        mix = [dext[k, strided] * (w[k] * w[k + 1]) for k in range(K - 1)]
        x = [
            [merged(tr[t, k, r], tr[t, K, r], k, 4, B - 4) for k in range(K)] for t in range(T)
        ]
        for t, solved in enumerate(solve(x, mix)):
            for k in range(K):
                ext[2 * K + t * K + k, strided] = solved[k]
    out_q.start()
    out_u.wait()
    out_v.wait()
    out_q.wait()


def computed(nlat, u, v, q, m, d, halos):
    any_space = pl.BlockSpec(memory_space=pl.ANY)
    return pl.pallas_call(
        functools.partial(compute, nlat),
        out_shape=(
            jax.ShapeDtypeStruct((K, B, B), F32),
            jax.ShapeDtypeStruct((K, B, B), F32),
            jax.ShapeDtypeStruct((T * K, B, B), F32),
        ),
        in_specs=[any_space] * 11,
        out_specs=[any_space] * 3,
        scratch_shapes=[
            pltpu.VMEM(((2 + T) * K, E, B), F32),
            pltpu.VMEM((K, E, B), jnp.int32),
            pltpu.VMEM((K - 1, E, B), F32),
            pltpu.VMEM((2, 2, E, B), F32),
            pltpu.VMEM((2, K + 1, R, 8, B), F32),
            pltpu.VMEM((2, K + 1, R, 8, B), F32),
            pltpu.VMEM((T, K + 1, R, 8, B), F32),
            pltpu.VMEM((K + 1, R, 8, B), F32),
            pltpu.VMEM((3, K + 1, R, 8, B), F32),
            pltpu.VMEM((3, K + 1, R, 8, B), F32),
            pltpu.VMEM((2, K + 1, 8, B), F32),
            pltpu.SemaphoreType.DMA((11,)),
            pltpu.SemaphoreType.DMA((3,)),
        ],
        compiler_params=pltpu.CompilerParams(vmem_limit_bytes=40 * 2**20),
    )(u, v, q, m, d, *halos)


def per_device(nlat, nlon, zonal_flow, meridional_flow, tracers, sea_mask, diffusivity):
    q = tracers.reshape(T * K, B, B)
    halos = exchanged(nlat, nlon, zonal_flow, meridional_flow, q, sea_mask)
    u, v, q = computed(nlat, zonal_flow, meridional_flow, q, sea_mask, diffusivity, halos)
    return u, v, q.reshape(T, K, B, B)


def solution(mesh):
    cells = P(None, "lat", "lon")
    traced = P(None, None, "lat", "lon")
    return jax.shard_map(
        functools.partial(per_device, mesh.shape["lat"], mesh.shape["lon"]),
        mesh=mesh,
        in_specs=(cells, cells, traced, cells, cells),
        out_specs=(cells, cells, traced),
        check_vma=False,
    )
```

```python
import functools
import math

import jax
import jax.numpy as jnp
from jax import lax
from jax.experimental import pallas as pl
from jax.experimental.pallas import tpu as pltpu
from jax.sharding import PartitionSpec as P

K = 4
T = 3
NSUB = 3
B = 128
H = 8
E = B + 2 * H
R = E // 8
S = 14
DEPTH = R
WET, U, V, Q = 4, 8, 12, 16
FIELDS = (WET, U, V, Q, Q + K, Q + 2 * K)
F32 = jnp.float32
MESH = pl.DeviceIdType.MESH
coriolis_peak = 0.5


def minmod(a, b):
    return jnp.maximum(jnp.minimum(a, b), jnp.minimum(jnp.maximum(a, b), 0.0))


def following(x):
    return pltpu.roll(x, B - 1, 1)


def preceding(x):
    return pltpu.roll(x, 1, 1)


def above(x):
    return pltpu.roll(x, 7, 0)


def below(x):
    return pltpu.roll(x, 1, 0)


def rolled(x, amount):
    return pltpu.roll(x, amount % B, 1) if amount % B else x


def flipped(x, index):
    x = jnp.take_along_axis(x, index, axis=1)
    backward = 7 - lax.broadcasted_iota(jnp.int32, (8, B), 0)
    return jnp.take_along_axis(x, backward, axis=0)


def solve(x, coupling):
    carried = []
    inverse = []
    for k in range(K):
        divisor = 1.0
        if k < K - 1:
            divisor = divisor + coupling[k]
        if k > 0:
            divisor = divisor + coupling[k - 1] * (1.0 - carried[k - 1])
        inverse.append(1.0 / divisor)
        if k < K - 1:
            carried.append(coupling[k] * inverse[k])
    results = []
    for field in x:
        scaled = [field[0] * inverse[0]]
        for k in range(1, K):
            scaled.append((field[k] + coupling[k - 1] * scaled[k - 1]) * inverse[k])
        solved = [scaled[K - 1]]
        for k in range(K - 2, -1, -1):
            solved.insert(0, scaled[k] + carried[k] * solved[0])
        results.append(solved)
    return results


def step(
    nlat, nlon, u, v, q, m, d, res,
    ext, mext, dext, hn, hs, hmn, hms, pe, pw, ke, kw, pn, flow, new, tr, wet, cx, cy, fold, load, send, recv,
):
    lat = lax.axis_index("lat")
    lon = lax.axis_index("lon")
    top = lat == nlat - 1
    bottom = lat == 0
    east = lax.rem(lon + 1, nlon)
    west = lax.rem(lon + nlon - 1, nlon)
    n_lat = jnp.where(top, lat, lat + 1)
    n_mid = jnp.where(top, nlon - 1 - lon, lon)
    n_west = jnp.where(top, lax.rem(nlon - lon, nlon), west)
    n_east = jnp.where(top, lax.rem(2 * nlon - 2 - lon, nlon), east)
    s_lat = jnp.maximum(lat - 1, 0)
    own_w = n_west == lon
    own_e = n_east == lon

    def at(row, column):
        return {"lat": row, "lon": column}

    middle = pl.ds(H, B)
    beyond = pl.ds(H + B, H)
    loads = [
        pltpu.make_async_copy(u, ext.at[U : U + K, middle], load.at[0]),
        pltpu.make_async_copy(v, ext.at[V : V + K, middle], load.at[1]),
        pltpu.make_async_copy(q, ext.at[Q : Q + T * K, middle], load.at[2]),
        pltpu.make_async_copy(m, mext, load.at[3]),
        pltpu.make_async_copy(d, dext.at[:, middle], load.at[4]),
    ]
    for copy in loads:
        copy.start()

    barrier = pltpu.get_barrier_semaphore()

    def greet(row, column):
        pl.semaphore_signal(barrier, inc=1, device_id=at(row, column), device_id_type=MESH)

    greet(lat, east)
    greet(lat, west)
    greet(n_lat, n_mid)

    @pl.when(jnp.logical_not(top & own_w))
    def _():
        greet(n_lat, n_west)

    @pl.when(jnp.logical_not(top & own_e))
    def _():
        greet(n_lat, n_east)

    @pl.when(jnp.logical_not(bottom))
    def _():
        greet(s_lat, lon)
        greet(s_lat, west)
        greet(s_lat, east)

    peers = (
        3
        + jnp.where(top & own_w, 0, 1)
        + jnp.where(top & own_e, 0, 1)
        + jnp.where(bottom, 0, 3)
    )
    pl.semaphore_wait(barrier, peers)

    def remote(src, dst, slot, row, column):
        return pltpu.make_async_remote_copy(
            src_ref=src,
            dst_ref=dst,
            send_sem=send.at[slot],
            recv_sem=recv.at[slot],
            device_id=at(row, column),
            device_id_type=MESH,
        )

    hi = pl.ds(B - H, H)
    lo = pl.ds(0, H)

    def rows(part, fields, marks, base, row, column):
        return [
            remote(u.at[:, part], fields.at[0:K], base, row, column),
            remote(v.at[:, part], fields.at[K : 2 * K], base + 1, row, column),
            remote(q.at[:, part], fields.at[2 * K :], base + 2, row, column),
            remote(m.at[:, part], marks, base + 3, row, column),
        ]

    to_north = rows(hi, hs, hms, 8, n_lat, n_mid)
    over_fold = rows(hi, hn, hmn, 2, n_lat, n_mid)
    to_south = rows(lo, hn, hmn, 2, s_lat, lon)

    @pl.when(top)
    def _():
        for copy in over_fold:
            copy.start()

    @pl.when(jnp.logical_not(top))
    def _():
        for copy in to_north:
            copy.start()

    @pl.when(jnp.logical_not(bottom))
    def _():
        for copy in to_south:
            copy.start()

    lane = lax.broadcasted_iota(jnp.int32, (8, B), 1)
    sub = lax.broadcasted_iota(jnp.int32, (8, B), 0)
    group = lane // 8
    for f in range(WET, Q + T * K):
        ext[f, lo] = jnp.zeros((H, B), F32)
        ext[f, beyond] = jnp.zeros((H, B), F32)
    for copy in loads:
        copy.wait()

    def pack(i, carry):
        part = pl.ds(pl.multiple_of(i * 8, 8), 8)
        held = pl.ds(pl.multiple_of(i * 8 + H, 8), 8)
        for k in range(K):
            ext[WET + k, held] = mext[k, part].astype(F32)
        for half in range(2):
            packed_w = jnp.zeros((8, B), F32)
            packed_e = jnp.zeros((8, B), F32)
            for k in range(K):
                for f, field in enumerate((Q, Q + K, Q + 2 * K, WET) if half == 0 else (U, V)):
                    x = ext[field + k, held]
                    j = 4 * k + f
                    x = pltpu.roll(x, 8 * j, 1) if j else x
                    packed_w = jnp.where(group == j, x, packed_w)
                    packed_e = jnp.where(group == (j - 1) % 16, x, packed_e)
            kw[half, part] = packed_w
            ke[half, part] = packed_e
        return carry

    lax.fori_loop(0, B // 8, pack, 0)

    sends = [
        remote(ke, pw.at[:, middle], 1, lat, east),
        remote(kw, pe.at[:, middle], 0, lat, west),
    ]
    for copy in sends:
        copy.start()
    north_east = remote(ke.at[:, hi], pw.at[:, lo], 13, n_lat, n_east)
    north_west = remote(kw.at[:, hi], pe.at[:, lo], 12, n_lat, n_west)
    fold_west = remote(kw.at[:, hi], pw.at[:, beyond], 7, n_lat, n_west)
    fold_east = remote(ke.at[:, hi], pe.at[:, beyond], 6, n_lat, n_east)
    self_west = pltpu.make_async_copy(kw.at[:, hi], pw.at[:, beyond], load.at[5])
    self_east = pltpu.make_async_copy(ke.at[:, hi], pe.at[:, beyond], load.at[6])
    south_east = remote(ke.at[:, lo], pw.at[:, beyond], 7, s_lat, east)
    south_west = remote(kw.at[:, lo], pe.at[:, beyond], 6, s_lat, west)

    @pl.when(jnp.logical_not(top))
    def _():
        north_east.start()
        north_west.start()

    @pl.when(top & own_w)
    def _():
        self_west.start()

    @pl.when(top & jnp.logical_not(own_w))
    def _():
        fold_west.start()

    @pl.when(top & own_e)
    def _():
        self_east.start()

    @pl.when(top & jnp.logical_not(own_e))
    def _():
        fold_east.start()

    @pl.when(jnp.logical_not(bottom))
    def _():
        south_east.start()
        south_west.start()

    place = lane % 32
    level = lane // 32
    far_hi = (place >= 10) & (place < 16)
    far_lo = (place >= 16) & (place < 22)
    is_hi = [(place < 10) & (level == k) for k in range(K)]
    is_lo = [(place >= 22) & (level == k) for k in range(K)]

    def edges(field, part):
        edge = jnp.zeros((8, B), F32)
        for k in range(K):
            x = ext[field + k, part]
            edge = jnp.where(is_hi[k], rolled(x, 32 * k + 10), edge)
            edge = jnp.where(is_lo[k], rolled(x, 32 * k + 22), edge)
        return edge

    def own_edges(i, carry):
        held = pl.ds(pl.multiple_of(i * 8 + H, 8), 8)
        for n, field in enumerate(FIELDS):
            pn[n, held] = edges(field, held)
        return carry

    lax.fori_loop(0, B // 8, own_edges, 0)

    def keep(n, i, r, x):
        if n == 0:
            wet[i, r] = x
        elif n < 3:
            flow[n - 1, i, r] = x
        else:
            tr[n - 3, i, r] = x

    def levels(n, r):
        for k in range(K):
            keep(n, k, r, ext[FIELDS[n] + k, pl.ds(r, 8, stride=R)])

    for r in range(R):
        for n in range(len(FIELDS)):
            levels(n, r)

    def coriolis(offset):
        row = lat * B + R * sub + lane - H
        ny = nlat * B
        return coriolis_peak * jnp.sin(math.pi * ((row.astype(F32) + offset) / ny - 0.5))

    cor_u = coriolis(0.5)
    cor_v = coriolis(1.0)

    def prepare(i, rows, count, bend, beyond_fold, momentum):
        def get(f, r):
            if r == -1:
                return below(flow[f, i, count - 1])
            if r == count:
                return above(flow[f, i, 0])
            return flow[f, i, r]

        us, vs = get(0, rows[0] - 1), get(1, rows[0] - 1)
        u0, v0 = get(0, rows[0]), get(1, rows[0])
        w0 = wet[i, rows[0]]
        for r in rows:
            un, vn = get(0, r + 1), get(1, r + 1)
            wn = wet[i, r + 1] if r < count - 1 else above(wet[i, 0])
            gu = w0 * following(w0)
            gv = w0 * wn
            ue = following(u0)
            ua = jnp.where(beyond_fold, ue, u0) if r > bend else u0
            va = jnp.where(beyond_fold, vn, v0) if r > bend else v0
            cx[0, i, r] = gu
            cx[1, i, r] = ua * gu
            cx[2, i, r] = jnp.where(ua > 0.0, 0.5, -0.5) - 0.5 * ua
            cy[0, i, r] = gv
            cy[1, i, r] = va * gv
            cy[2, i, r] = jnp.where(va > 0.0, 0.5, -0.5) - 0.5 * va
            if r == bend:
                vf = jnp.where(beyond_fold, vn, v0)
                fold[0, i] = vf * gv
                fold[1, i] = jnp.where(vf > 0.0, 0.5, -0.5) - 0.5 * vf
            if momentum:
                a = v0 + vs
                vbar = 0.25 * (a + following(a))
                a = u0 + un
                ubar = 0.25 * (a + preceding(a))
                fu = jnp.broadcast_to(cor_u[:, r : r + 1], (8, B))
                fv = jnp.broadcast_to(cor_v[:, r : r + 1], (8, B))
                du = vbar * (fu - 0.5 * (un - us)) - 0.5 * u0 * (ue - preceding(u0))
                dv = -ubar * (fv + 0.5 * (following(v0) - preceding(v0))) - 0.5 * v0 * (vn - vs)
                new[0, i, r] = u0 + gu * du
                new[1, i, r] = v0 + gv * dv
            us, vs, u0, v0, w0 = u0, v0, un, vn, wn

    last = top & (sub == 7)
    last_strip = top & (sub >= 4)
    bend = R - H - 1

    def prepare_level(rows, i, carry):
        prepare(i, rows, R, bend, last, True)
        return carry

    lax.fori_loop(0, K, functools.partial(prepare_level, range(R)), 0)

    def face(w, c, here, there, slope_here, slope_there):
        way = w > 0.0
        return w * (jnp.where(way, here, there) + c * jnp.where(way, slope_here, slope_there))

    def advect(i, count, bend):
        turned, last_jump, last_slope = [], [], []
        now, ahead, jump, slope, south = [], [], [], [], []
        for t in range(T):
            x0, x1 = tr[t, i, 0], tr[t, i, 1]
            xr = above(x0)
            jr = (xr - tr[t, i, count - 1]) * cy[0, i, count - 1]
            j0 = (x1 - x0) * cy[0, i, 0]
            s0 = minmod(j0, below(jr))
            turned.append(xr)
            last_jump.append(jr)
            last_slope.append(above(s0))
            now.append(x0)
            ahead.append(x1)
            jump.append(j0)
            slope.append(s0)
            south.append(None)
        state = {}

        def stage_a(t, r):
            x, xn = now[t], ahead[t]
            if r + 1 < count - 1:
                xnn = tr[t, i, r + 2]
                jn = (xnn - xn) * cy[0, i, r + 1]
                sn = minmod(jn, jump[t])
            elif r + 1 == count - 1:
                xnn = turned[t]
                jn = last_jump[t]
                sn = minmod(jn, jump[t])
            else:
                xnn = jn = None
                sn = last_slope[t]
            north = face(cy[1, i, r], cy[2, i, r], x, xn, slope[t], sn)
            e = following(x)
            y = x - north if r == 0 else x - (north - south[t])
            if r == bend:
                north = face(fold[0, i], fold[1, i], x, xn, slope[t], sn)
            south[t] = north
            now[t], ahead[t], jump[t], slope[t] = xn, xnn, jn, sn
            state[t, r] = (x, e, y)

        def stage_b(t, r):
            x, e, y = state[t, r]
            j = (e - x) * cx[0, i, r]
            state[t, r] = (x, e, y, j, preceding(j))

        def stage_c(t, r):
            x, e, y, j, jp = state[t, r]
            s = minmod(j, jp)
            state[t, r] = (x, e, y, s, following(s))

        def stage_d(t, r):
            x, e, y, s, sn = state[t, r]
            f = face(cx[1, i, r], cx[2, i, r], x, e, s, sn)
            state[t, r] = (y - f, preceding(f))

        def stage_e(t, r):
            y, fp = state.pop((t, r))
            y = y + fp
            tr[t, i, r] = y

        stages = [stage_a, stage_b, stage_c, stage_d, stage_e]
        for tick in range(count + 4 * DEPTH):
            for n in (4, 3, 2, 1, 0):
                r = tick - n * DEPTH
                if 0 <= r < count:
                    for t in range(T):
                        stages[n](t, r)
        for t in range(T):
            tr[t, i, 0] = tr[t, i, 0] + below(south[t])

    def advect_level(i, carry):
        advect(lax.rem(i, K + 1), R, bend)
        return carry

    def advect_inner(i, carry):
        advect(lax.rem(i, K), R, bend)
        return carry

    lax.fori_loop(0, 2 * K, advect_inner, 0)

    for copy in sends:
        copy.wait_send()

    @pl.when(top)
    def _():
        for copy in over_fold:
            copy.wait_send()

    @pl.when(jnp.logical_not(top))
    def _():
        for copy in to_north:
            copy.wait_send()
        north_east.wait_send()
        north_west.wait_send()

    @pl.when(top & own_w)
    def _():
        self_west.wait()

    @pl.when(top & jnp.logical_not(own_w))
    def _():
        fold_west.wait_send()

    @pl.when(top & own_e)
    def _():
        self_east.wait()

    @pl.when(top & jnp.logical_not(own_e))
    def _():
        fold_east.wait_send()

    @pl.when(jnp.logical_not(bottom))
    def _():
        for copy in to_south:
            copy.wait_send()
        south_east.wait_send()
        south_west.wait_send()

    for copy in sends:
        copy.wait_recv()
    for copy in to_south:
        copy.wait_recv()

    @pl.when(jnp.logical_not(top & own_w))
    def _():
        south_east.wait_recv()

    @pl.when(jnp.logical_not(top & own_e))
    def _():
        south_west.wait_recv()

    @pl.when(jnp.logical_not(bottom))
    def _():
        for copy in to_north:
            copy.wait_recv()
        north_east.wait_recv()
        north_west.wait_recv()


    for n, field in enumerate((U, V, Q, Q + K, Q + 2 * K)):
        for k in range(K):
            ext[field + k, lo] = hs[n * K + k]
            ext[field + k, beyond] = hn[n * K + k]
    for k in range(K):
        ext[WET + k, lo] = hms[k].astype(F32)
        ext[WET + k, beyond] = hmn[k].astype(F32)

    @pl.when(bottom)
    def _():
        for f in range(WET, Q + T * K):
            ext[f, lo] = jnp.zeros((H, B), F32)
        for half in range(2):
            pe[half, lo] = jnp.zeros((H, B), F32)
            pw[half, lo] = jnp.zeros((H, B), F32)

    @pl.when(top)
    def _():
        whole = B - 1 - lane
        for f in range(WET, Q + T * K):
            x = flipped(ext[f, beyond], whole)
            ext[f, beyond] = -x if U <= f < Q else x
        within = 7 - lane % 8
        from_east = (lane // 8 + 15) % 16 * 8 + within
        from_west = (lane // 8 + 1) % 16 * 8 + within
        for half in range(2):
            x = flipped(pe[half, beyond], from_east)
            pe[half, beyond] = -x if half else x
            x = flipped(pw[half, beyond], from_west)
            pw[half, beyond] = -x if half else x

    for n, field in enumerate(FIELDS):
        pn[n, lo] = edges(field, lo)
        pn[n, beyond] = edges(field, beyond)
    for i in range(R):
        part = pl.ds(8 * i, 8)
        for n in range(len(FIELDS)):
            half, slot = ((0, 3), (1, 0), (1, 1), (0, 0), (0, 1), (0, 2))[n]
            x = jnp.where(far_hi, rolled(pe[half, part], 10 - 8 * slot), pn[n, part])
            pn[n, part] = jnp.where(far_lo, rolled(pw[half, part], 22 - 8 * slot), x)
    for r in range(R):
        for n in range(len(FIELDS)):
            keep(n, K, r, pn[n, pl.ds(r, 8, stride=R)])

    flat = ext.reshape(32 * E, B)
    for r in range(S):
        for n, field in enumerate(FIELDS):
            south_rows = flat[pl.ds(field * E + H - 6 + r, 8, stride=E), :]
            north_rows = flat[pl.ds((field - K) * E + H + 120 + r, 8, stride=E), :]
            keep(n, K + 1, r, jnp.where(sub < 4, south_rows, north_rows))

    for r in (6, 7, 10, 11):
        for n in range(3):
            levels(n, r)
    prepare(K, range(R), R, bend, last, True)
    prepare(K + 1, range(S), S, 7, last_strip, False)
    lax.fori_loop(0, K, functools.partial(prepare_level, range(6, 11)), 0)

    def advect_edges(i, carry):
        advect(K, R, bend)
        advect(K + 1, S, 7)
        return carry

    lax.fori_loop(0, 2, advect_edges, 0)

    def merged(x, edge, k, low, high):
        source = jnp.where(lane < B // 2, lane + 32 * k + 22, lane + 32 * k + 10) % B
        edge = jnp.take_along_axis(edge, source, axis=1)
        return jnp.where((lane < low) | (lane >= high), edge, x)

    ends = (sub == 0) | (sub == 7)
    for t in range(T):
        for k in range(K):
            source = jnp.where(sub == 0, k, 4 + k)
            for r in range(R):
                x = tr[t, k, r]
                if 6 <= r < 12:
                    x = jnp.where(ends, jnp.take_along_axis(tr[t, K + 1, r - 2], source, axis=0), x)
                tr[t, k, r] = merged(x, tr[t, K, r], k, 4, B - 4)

    lax.fori_loop(0, K + 1, advect_level, 0)

    for r in range(R):
        strided = pl.ds(r, 8, stride=R)
        mix = [dext[k, strided] for k in range(K - 1)]
        gu = [merged(cx[0, k, r], cx[0, K, r], k, 0, B - 1) for k in range(K)]
        gv = [cy[0, k, r] for k in range(K)]
        un = [merged(new[0, k, r], new[0, K, r], k, 1, B - 1) for k in range(K)]
        vn = [merged(new[1, k, r], new[1, K, r], k, 1, B - 1) for k in range(K)]
        (un,) = solve([un], [mix[k] * (gu[k] * gu[k + 1]) for k in range(K - 1)])
        (vn,) = solve([vn], [mix[k] * (gv[k] * gv[k + 1]) for k in range(K - 1)])
        for k in range(K):
            res[k, strided] = un[k]
            res[K + k, strided] = vn[k]
        w = [wet[k, r] for k in range(K)]
        mix = [mix[k] * (w[k] * w[k + 1]) for k in range(K - 1)]
        x = [
            [merged(tr[t, k, r], tr[t, K, r], k, 2, B - 2) for k in range(K)] for t in range(T)
        ]
        for t, solved in enumerate(solve(x, mix)):
            for k in range(K):
                res[2 * K + t * K + k, strided] = solved[k]


def stepped(nlat, nlon, u, v, q, m, d):
    hbm = pl.BlockSpec(memory_space=pltpu.HBM)
    return pl.pallas_call(
        functools.partial(step, nlat, nlon),
        out_shape=jax.ShapeDtypeStruct(((2 + T) * K, E, B), F32),
        in_specs=[hbm] * 5,
        out_specs=pl.BlockSpec(memory_space=pltpu.VMEM),
        scratch_shapes=[
            pltpu.VMEM((32, E, B), F32),
            pltpu.VMEM((K, B, B), jnp.int32),
            pltpu.VMEM((K - 1, E, B), F32),
            pltpu.VMEM(((2 + T) * K, H, B), F32),
            pltpu.VMEM(((2 + T) * K, H, B), F32),
            pltpu.VMEM((K, H, B), jnp.int32),
            pltpu.VMEM((K, H, B), jnp.int32),
            pltpu.VMEM((2, E, B), F32),
            pltpu.VMEM((2, E, B), F32),
            pltpu.VMEM((2, B, B), F32),
            pltpu.VMEM((2, B, B), F32),
            pltpu.VMEM((len(FIELDS), E, B), F32),
            pltpu.VMEM((2, K + 2, R, 8, B), F32),
            pltpu.VMEM((2, K + 1, R, 8, B), F32),
            pltpu.VMEM((T, K + 2, R, 8, B), F32),
            pltpu.VMEM((K + 2, R, 8, B), F32),
            pltpu.VMEM((3, K + 2, R, 8, B), F32),
            pltpu.VMEM((3, K + 2, R, 8, B), F32),
            pltpu.VMEM((2, K + 2, 8, B), F32),
            pltpu.SemaphoreType.DMA((7,)),
            pltpu.SemaphoreType.DMA((14,)),
            pltpu.SemaphoreType.DMA((14,)),
        ],
        compiler_params=pltpu.CompilerParams(
            collective_id=0, has_side_effects=True, vmem_limit_bytes=40 * 2**20
        ),
    )(u, v, q, m, d)


def deliver(res, u, v, q, done):
    middle = pl.ds(H, B)
    copies = [
        pltpu.make_async_copy(res.at[0:K, middle], u, done.at[0]),
        pltpu.make_async_copy(res.at[K : 2 * K, middle], v, done.at[1]),
        pltpu.make_async_copy(res.at[2 * K :, middle], q, done.at[2]),
    ]
    for copy in copies:
        copy.start()
    for copy in copies:
        copy.wait()


def delivered(res):
    return pl.pallas_call(
        deliver,
        out_shape=(
            jax.ShapeDtypeStruct((K, B, B), F32),
            jax.ShapeDtypeStruct((K, B, B), F32),
            jax.ShapeDtypeStruct((T * K, B, B), F32),
        ),
        in_specs=[pl.BlockSpec(memory_space=pltpu.VMEM)],
        out_specs=[pl.BlockSpec(memory_space=pltpu.HBM)] * 3,
        scratch_shapes=[pltpu.SemaphoreType.DMA((3,))],
    )(res)


def per_device(nlat, nlon, zonal_flow, meridional_flow, tracers, sea_mask, diffusivity):
    q = tracers.reshape(T * K, B, B)
    given = [
        pltpu.with_memory_space_constraint(x, pltpu.HBM)
        for x in (zonal_flow, meridional_flow, q, sea_mask, diffusivity)
    ]
    res = pltpu.with_memory_space_constraint(stepped(nlat, nlon, *given), pltpu.VMEM)
    u, v, q = delivered(res)
    return u, v, q.reshape(T, K, B, B)


def solution(mesh):
    cells = P(None, "lat", "lon")
    traced = P(None, None, "lat", "lon")
    return jax.shard_map(
        functools.partial(per_device, mesh.shape["lat"], mesh.shape["lon"]),
        mesh=mesh,
        in_specs=(cells, cells, traced, cells, cells),
        out_specs=(cells, cells, traced),
        check_vma=False,
    )
```

```python
import functools
import math

import jax
import jax.numpy as jnp
from jax import lax
from jax.experimental import pallas as pl
from jax.experimental.pallas import tpu as pltpu
from jax.sharding import PartitionSpec as P

K = 4
T = 3
NSUB = 3
B = 128
H = 8
E = B + 2 * H
R = E // 8
S = 14
DEPTH = R
WET, U, V, Q = 4, 8, 12, 16
FIELDS = (WET, U, V, Q, Q + K, Q + 2 * K)
F32 = jnp.float32
MESH = pl.DeviceIdType.MESH
coriolis_peak = 0.5


def flush(pending):
    for ref, index, x in pending:
        ref[index] = x
    pending.clear()


class Batch:
    def __init__(self, parts):
        self.parts = list(parts)

    def __add__(self, other):
        return each(jnp.add, self, other)

    __radd__ = __add__

    def __sub__(self, other):
        return each(jnp.subtract, self, other)

    def __rsub__(self, other):
        return each(jnp.subtract, other, self)

    def __mul__(self, other):
        return each(jnp.multiply, self, other)

    __rmul__ = __mul__

    def __rtruediv__(self, other):
        return each(jnp.divide, other, self)

    def __neg__(self):
        return each(jnp.negative, self)

    def __gt__(self, other):
        return each(jnp.greater, self, other)


def each(function, *given):
    size = [len(x.parts) for x in given if isinstance(x, Batch)]
    if not size:
        return function(*given)
    return Batch(
        function(*(x.parts[n] if isinstance(x, Batch) else x for x in given)) for n in range(size[0])
    )


def where(mask, a, b):
    return each(jnp.where, mask, a, b)


def minmod(a, b):
    return each(jnp.maximum, each(jnp.minimum, a, b), each(jnp.minimum, each(jnp.maximum, a, b), 0.0))


def following(x):
    return each(lambda part: pltpu.roll(part, B - 1, 1), x)


def preceding(x):
    return each(lambda part: pltpu.roll(part, 1, 1), x)


def above(x):
    return pltpu.roll(x, 7, 0)


def below(x):
    return pltpu.roll(x, 1, 0)


def rolled(x, amount):
    return each(lambda part: pltpu.roll(part, amount % B, 1), x) if amount % B else x


def picked(x, index):
    return each(lambda part: jnp.take_along_axis(part, index, axis=1), x)


def flipped(x, index):
    x = jnp.take_along_axis(x, index, axis=1)
    backward = 7 - lax.broadcasted_iota(jnp.int32, (8, B), 0)
    return jnp.take_along_axis(x, backward, axis=0)


def solve(x, coupling):
    carried = []
    inverse = []
    for k in range(K):
        divisor = 1.0
        if k < K - 1:
            divisor = divisor + coupling[k]
        if k > 0:
            divisor = divisor + coupling[k - 1] * (1.0 - carried[k - 1])
        inverse.append(1.0 / divisor)
        if k < K - 1:
            carried.append(coupling[k] * inverse[k])
    results = []
    for field in x:
        scaled = [field[0] * inverse[0]]
        for k in range(1, K):
            scaled.append((field[k] + coupling[k - 1] * scaled[k - 1]) * inverse[k])
        solved = [scaled[K - 1]]
        for k in range(K - 2, -1, -1):
            solved.insert(0, scaled[k] + carried[k] * solved[0])
        results.append(solved)
    return results


def step(
    nlat, nlon, u, v, q, m, d, res,
    ext, mext, dext, hn, hs, hmn, hms, pe, pw, ke, kw, pn, flow, new, tr, wet, cx, cy, fold, cor, load, send, recv,
):
    lat = lax.axis_index("lat")
    lon = lax.axis_index("lon")
    top = lat == nlat - 1
    bottom = lat == 0
    east = lax.rem(lon + 1, nlon)
    west = lax.rem(lon + nlon - 1, nlon)
    n_lat = jnp.where(top, lat, lat + 1)
    n_mid = jnp.where(top, nlon - 1 - lon, lon)
    n_west = jnp.where(top, lax.rem(nlon - lon, nlon), west)
    n_east = jnp.where(top, lax.rem(2 * nlon - 2 - lon, nlon), east)
    s_lat = jnp.maximum(lat - 1, 0)
    own_w = n_west == lon
    own_e = n_east == lon

    def at(row, column):
        return {"lat": row, "lon": column}

    middle = pl.ds(H, B)
    beyond = pl.ds(H + B, H)
    loads = [
        pltpu.make_async_copy(u, ext.at[U : U + K, middle], load.at[0]),
        pltpu.make_async_copy(v, ext.at[V : V + K, middle], load.at[1]),
        pltpu.make_async_copy(q, ext.at[Q : Q + T * K, middle], load.at[2]),
        pltpu.make_async_copy(m, mext, load.at[3]),
        pltpu.make_async_copy(d, dext.at[:, middle], load.at[4]),
    ]
    for copy in loads:
        copy.start()

    barrier = pltpu.get_barrier_semaphore()

    def greet(row, column):
        pl.semaphore_signal(barrier, inc=1, device_id=at(row, column), device_id_type=MESH)

    greet(lat, east)
    greet(lat, west)
    greet(n_lat, n_mid)

    @pl.when(jnp.logical_not(top & own_w))
    def _():
        greet(n_lat, n_west)

    @pl.when(jnp.logical_not(top & own_e))
    def _():
        greet(n_lat, n_east)

    @pl.when(jnp.logical_not(bottom))
    def _():
        greet(s_lat, lon)
        greet(s_lat, west)
        greet(s_lat, east)

    def remote(src, dst, slot, row, column):
        return pltpu.make_async_remote_copy(
            src_ref=src,
            dst_ref=dst,
            send_sem=send.at[slot],
            recv_sem=recv.at[slot],
            device_id=at(row, column),
            device_id_type=MESH,
        )

    hi = pl.ds(B - H, H)
    lo = pl.ds(0, H)
    lo_held = pl.ds(H, H)
    hi_held = pl.ds(B, H)

    def rows(part, fields, marks, base, row, column):
        return [
            remote(u.at[:, part], fields.at[0:K], base, row, column),
            remote(v.at[:, part], fields.at[K : 2 * K], base + 1, row, column),
            remote(q.at[:, part], fields.at[2 * K :], base + 2, row, column),
            remote(m.at[:, part], marks, base + 3, row, column),
        ]

    to_north = rows(hi, hs, hms, 8, n_lat, n_mid)
    over_fold = rows(hi, hn, hmn, 2, n_lat, n_mid)
    to_south = rows(lo, hn, hmn, 2, s_lat, lon)

    def enter():
        peers = (
            3
            + jnp.where(top & own_w, 0, 1)
            + jnp.where(top & own_e, 0, 1)
            + jnp.where(bottom, 0, 3)
        )
        pl.semaphore_wait(barrier, peers)

        @pl.when(top)
        def _():
            for copy in over_fold:
                copy.start()

        @pl.when(jnp.logical_not(top))
        def _():
            for copy in to_north:
                copy.start()

        @pl.when(jnp.logical_not(bottom))
        def _():
            for copy in to_south:
                copy.start()

    reached_late = lon >= nlon // 2

    @pl.when(reached_late)
    def _():
        enter()

    lane = lax.broadcasted_iota(jnp.int32, (8, B), 1)
    sub = lax.broadcasted_iota(jnp.int32, (8, B), 0)
    group = lane // 8
    own_rows, lo_pack, hi_pack = pl.ds(H, B), pl.ds(0, 2 * H), pl.ds(B, 2 * H)
    lo_land, mid_land, hi_land = pl.ds(0, 2 * H), pl.ds(2 * H, B), pl.ds(2 * H + B, 2 * H)
    sends = [
        remote(ke.at[own_rows], pw.at[mid_land], 1, lat, east),
        remote(kw.at[own_rows], pe.at[mid_land], 0, lat, west),
    ]
    north_east = remote(ke.at[hi_pack], pw.at[lo_land], 13, n_lat, n_east)
    north_west = remote(kw.at[hi_pack], pe.at[lo_land], 12, n_lat, n_west)
    fold_west = remote(kw.at[hi_pack], pw.at[hi_land], 7, n_lat, n_west)
    fold_east = remote(ke.at[hi_pack], pe.at[hi_land], 6, n_lat, n_east)
    self_west = pltpu.make_async_copy(kw.at[hi_pack], pw.at[hi_land], load.at[5])
    self_east = pltpu.make_async_copy(ke.at[hi_pack], pe.at[hi_land], load.at[6])
    south_east = remote(ke.at[lo_pack], pw.at[hi_land], 7, s_lat, east)
    south_west = remote(kw.at[lo_pack], pe.at[hi_land], 6, s_lat, west)

    for f in range(WET, Q + T * K):
        ext[f, lo] = jnp.zeros((H, B), F32)
        ext[f, beyond] = jnp.zeros((H, B), F32)
    for copy in loads:
        copy.wait()

    place = lane % 32
    level = lane // 32
    spare_w = (place == 6) | (place == 7) | (place == 14) | (place == 15)
    spare_e = (place == 0) | (place == 1) | (place == 8) | (place == 9)
    spare_of = jnp.where(
        spare_w,
        jnp.where(place < 8, place - 6, place - 12),
        jnp.where(place < 8, B - 4 + place, B - 10 + place),
    )
    spare_of = jnp.minimum(spare_of, B - 1)

    blocks = [pl.ds(i * 8, 8) for i in range(B // 8)]
    held_blocks = [pl.ds(i * 8 + H, 8) for i in range(B // 8)]

    def read(ref, *index):
        return Batch(ref[(*index, part)] for part in held_blocks)

    pending = []

    def write(ref, index, x):
        for part, y in zip(held_blocks, x.parts, strict=True):
            pending.append((ref, (*index, part), y))

    packed_w = packed_e = Batch([jnp.zeros((8, B), F32)] * len(blocks))
    for k in range(K):
        sea = Batch(mext[k, part].astype(F32) for part in blocks)
        write(ext, (WET + k,), sea)
        for f in range(T + 1):
            j = 4 * k + f
            x = rolled(read(ext, Q + f * K + k) if f < T else sea, 8 * j)
            packed_w = where(group == j, x, packed_w)
            packed_e = where(group == (j - 1) % 16, x, packed_e)
        x = picked(read(ext, V + k), spare_of)
        packed_w = where(spare_w & (level == k), x, packed_w)
        packed_e = where(spare_e & (level == k), x, packed_e)
    write(kw, (), packed_w)
    write(ke, (), packed_e)
    flush(pending)
    for first, held in ((0, lo_held), (B + H, hi_held)):
        packed_w = jnp.zeros((8, B), F32)
        packed_e = jnp.zeros((8, B), F32)
        for k in range(K):
            for f, field in enumerate((U, V)):
                j = 4 * k + f
                x = rolled(ext[field + k, held], 8 * j)
                packed_w = jnp.where(group == j, x, packed_w)
                packed_e = jnp.where(group == (j - 1) % 16, x, packed_e)
        kw[pl.ds(first, 8)] = packed_w
        ke[pl.ds(first, 8)] = packed_e

    def enter_columns():
        @pl.when(jnp.logical_not(top))
        def _():
            north_east.start()
            north_west.start()

        @pl.when(top & own_w)
        def _():
            self_west.start()

        @pl.when(top & jnp.logical_not(own_w))
        def _():
            fold_west.start()

        @pl.when(top & own_e)
        def _():
            self_east.start()

        @pl.when(top & jnp.logical_not(own_e))
        def _():
            fold_east.start()

        @pl.when(jnp.logical_not(bottom))
        def _():
            south_east.start()
            south_west.start()

        for copy in sends:
            copy.start()

    @pl.when(reached_late)
    def _():
        enter_columns()

    far_hi = (place >= 10) & (place < 16)
    far_lo = (place >= 16) & (place < 22)
    source_of = (place + jnp.where(place < 16, 118, B - 22)) % B

    def edges(field, parts):
        edge = picked(Batch(ext[field, part] for part in parts), source_of)
        for k in range(1, K):
            x = picked(Batch(ext[field + k, part] for part in parts), source_of)
            edge = where(level == k, x, edge)
        return edge

    for n, field in enumerate(FIELDS):
        write(pn, (n,), edges(field, held_blocks))
        flush(pending)

    def keep(n, i, r, x):
        ref, index = (wet, (i, r)) if n == 0 else (flow, (n - 1, i, r)) if n < 3 else (tr, (n - 3, i, r))
        pending.append((ref, index, x))

    def levels(n, r):
        for k in range(K):
            keep(n, k, r, ext[FIELDS[n] + k, pl.ds(r, 8, stride=R)])

    for r in range(R):
        for n in range(len(FIELDS)):
            levels(n, r)
        flush(pending)

    @pl.when(jnp.logical_not(reached_late))
    def _():
        enter()
        enter_columns()

    def coriolis(offset):
        row = lat * B + R * sub + lane - H
        ny = nlat * B
        return coriolis_peak * jnp.sin(math.pi * ((row.astype(F32) + offset) / ny - 0.5))

    for f, offset in enumerate((0.5, 1.0)):
        turning = coriolis(offset)
        for r in range(R):
            cor[f, r] = jnp.broadcast_to(turning[:, r : r + 1], (8, B))

    def prepare(i, rows, count, bend, beyond_fold, momentum):
        def get(f, r):
            if r == -1:
                return below(flow[f, i, count - 1])
            if r == count:
                return above(flow[f, i, 0])
            return flow[f, i, r]

        for start in range(0, len(rows), 9):
            chunk = rows[start : start + 9]

            def put(ref, index, x):
                for r, y in zip(chunk, x.parts, strict=True):
                    held_back.append((ref, (index, i, r), y))

            def bent(a, b):
                return Batch(
                    jnp.where(beyond_fold, x, y) if r > bend else y
                    for r, x, y in zip(chunk, a.parts, b.parts, strict=True)
                )

            held_back = []
            u0, v0 = (Batch(get(f, r) for r in chunk) for f in range(2))
            un, vn = (Batch(get(f, r + 1) for r in chunk) for f in range(2))
            w0 = Batch(wet[i, r] for r in chunk)
            wn = Batch(wet[i, r + 1] if r < count - 1 else above(wet[i, 0]) for r in chunk)
            gu = w0 * following(w0)
            gv = w0 * wn
            ue = following(u0)
            uw = preceding(u0)
            gw = preceding(gu)
            ua = bent(ue, u0)
            wa = bent(u0, uw)
            va = bent(vn, v0)
            put(cx, 0, gu)
            put(cx, 1, each(jnp.maximum, ua, 0.0) * gu)
            put(cx, 2, 0.5 - 0.5 * ua)
            put(cx, 3, gw)
            put(cx, 4, each(jnp.minimum, wa, 0.0) * gw)
            put(cx, 5, -0.5 - 0.5 * wa)
            put(cy, 0, gv)
            put(cy, 1, va * gv)
            put(cy, 2, where(va > 0.0, 0.5, -0.5) - 0.5 * va)
            if bend in chunk:
                n = chunk.index(bend)
                vf = jnp.where(beyond_fold, vn.parts[n], v0.parts[n])
                held_back.append((fold, (0, i), vf * gv.parts[n]))
                held_back.append((fold, (1, i), jnp.where(vf > 0.0, 0.5, -0.5) - 0.5 * vf))
            if momentum:
                us, vs = (Batch(get(f, r - 1) for r in chunk) for f in range(2))
                turn_u, turn_v = (Batch(cor[f, r] for r in chunk) for f in range(2))
                a = v0 + vs
                vbar = 0.25 * (a + following(a))
                a = u0 + un
                ubar = 0.25 * (a + preceding(a))
                du = vbar * (turn_u - 0.5 * (un - us)) - 0.5 * u0 * (ue - uw)
                dv = -ubar * (turn_v + 0.5 * (following(v0) - preceding(v0))) - 0.5 * v0 * (vn - vs)
                put(new, 0, u0 + gu * du)
                put(new, 1, v0 + gv * dv)
            flush(held_back)

    last = top & (sub == 7)
    last_strip = top & (sub >= 4)
    bend = R - H - 1

    def prepare_level(rows, i, carry):
        prepare(i, rows, R, bend, last, True)
        return carry

    lax.fori_loop(0, K, functools.partial(prepare_level, range(R)), 0)

    def face(w, c, here, there, slope_here, slope_there):
        way = w > 0.0
        return w * (jnp.where(way, here, there) + c * jnp.where(way, slope_here, slope_there))

    def advect(i, count, bend):
        first, held_back = [None] * T, []
        turned, last_jump, last_slope = [], [], []
        now, ahead, jump, slope, south = [], [], [], [], []
        for t in range(T):
            x0, x1 = tr[t, i, 0], tr[t, i, 1]
            xr = above(x0)
            jr = (xr - tr[t, i, count - 1]) * cy[0, i, count - 1]
            j0 = (x1 - x0) * cy[0, i, 0]
            s0 = minmod(j0, below(jr))
            turned.append(xr)
            last_jump.append(jr)
            last_slope.append(above(s0))
            now.append(x0)
            ahead.append(x1)
            jump.append(j0)
            slope.append(s0)
            south.append(None)
        state = {}

        def stage_a(t, r):
            x = tr[t, i, r]
            state[t, r] = (following(x), preceding(x))

        def stage_b(t, r):
            e, p = state[t, r]
            x = tr[t, i, r]
            s = minmod((e - x) * cx[0, i, r], (x - p) * cx[3, i, r])
            a = cx[1, i, r] * (x + cx[2, i, r] * s)
            b = cx[4, i, r] * (x + cx[5, i, r] * s)
            state[t, r] = (b - a, preceding(a), following(b))

        def stage_e(t, r):
            own, a, b = state.pop((t, r))
            x, xn = now[t], ahead[t]
            if r + 1 < count - 1:
                xnn = tr[t, i, r + 2]
                jn = (xnn - xn) * cy[0, i, r + 1]
                sn = minmod(jn, jump[t])
            elif r + 1 == count - 1:
                xnn = turned[t]
                jn = last_jump[t]
                sn = minmod(jn, jump[t])
            else:
                xnn = jn = None
                sn = last_slope[t]
            north = face(cy[1, i, r], cy[2, i, r], x, xn, slope[t], sn)
            y = x - north if r == 0 else x - (north - south[t])
            if r == bend:
                north = face(fold[0, i], fold[1, i], x, xn, slope[t], sn)
            south[t] = north
            now[t], ahead[t], jump[t], slope[t] = xn, xnn, jn, sn
            y = y + (own + (a - b))
            if r == 0:
                first[t] = y
            else:
                held_back.append((tr, (t, i, r), y))

        stages = [stage_a, stage_b, stage_e]
        for tick in range(count + 2 * DEPTH):
            for n in (2, 1, 0):
                r = tick - n * DEPTH
                if 0 <= r < count:
                    for t in range(T):
                        stages[n](t, r)
            if tick % 3 == 2:
                flush(held_back)
        flush(held_back)
        for t in range(T):
            tr[t, i, 0] = first[t] + below(south[t])

    def advect_level(i, carry):
        advect(lax.rem(i, K + 1), R, bend)
        return carry

    def advect_inner(i, carry):
        advect(lax.rem(i, K), R, bend)
        return carry

    lax.fori_loop(0, 2 * K, advect_inner, 0)

    for copy in sends:
        copy.wait_send()

    @pl.when(top)
    def _():
        for copy in over_fold:
            copy.wait_send()

    @pl.when(jnp.logical_not(top))
    def _():
        for copy in to_north:
            copy.wait_send()
        north_east.wait_send()
        north_west.wait_send()

    @pl.when(top & own_w)
    def _():
        self_west.wait()

    @pl.when(top & jnp.logical_not(own_w))
    def _():
        fold_west.wait_send()

    @pl.when(top & own_e)
    def _():
        self_east.wait()

    @pl.when(top & jnp.logical_not(own_e))
    def _():
        fold_east.wait_send()

    @pl.when(jnp.logical_not(bottom))
    def _():
        for copy in to_south:
            copy.wait_send()
        south_east.wait_send()
        south_west.wait_send()

    for copy in sends:
        copy.wait_recv()
    for copy in to_south:
        copy.wait_recv()

    @pl.when(jnp.logical_not(top & own_w))
    def _():
        south_east.wait_recv()

    @pl.when(jnp.logical_not(top & own_e))
    def _():
        south_west.wait_recv()

    @pl.when(jnp.logical_not(bottom))
    def _():
        for copy in to_north:
            copy.wait_recv()
        north_east.wait_recv()
        north_west.wait_recv()


    for n, field in enumerate((U, V, Q, Q + K, Q + 2 * K)):
        for k in range(K):
            pending.append((ext, (field + k, lo), hs[n * K + k]))
            pending.append((ext, (field + k, beyond), hn[n * K + k]))
    for k in range(K):
        pending.append((ext, (WET + k, lo), hms[k].astype(F32)))
        pending.append((ext, (WET + k, beyond), hmn[k].astype(F32)))
    flush(pending)

    @pl.when(bottom)
    def _():
        for f in range(WET, Q + T * K):
            ext[f, lo] = jnp.zeros((H, B), F32)
        pe[lo_land] = jnp.zeros((2 * H, B), F32)
        pw[lo_land] = jnp.zeros((2 * H, B), F32)

    @pl.when(top)
    def _():
        whole = B - 1 - lane
        turned = [flipped(ext[f, beyond], whole) for f in range(WET, Q + T * K)]
        for f, x in enumerate(turned, WET):
            ext[f, beyond] = -x if U <= f < Q else x
        within = 7 - lane % 8
        from_east = (lane // 8 + 15) % 16 * 8 + within
        from_west = (lane // 8 + 1) % 16 * 8 + within
        first, second = pl.ds(2 * H + B, H), pl.ds(3 * H + B, H)
        for landed, source in ((pe, from_east), (pw, from_west)):
            x, y = flipped(landed[first], source), flipped(landed[second], source)
            landed[first] = -y
            landed[second] = x

    def spread(n, parts, pack_e, pack_w, slot, own):
        x = where(far_hi, rolled(pack_e, 10 - 8 * slot), own)
        x = where(far_lo, rolled(pack_w, 22 - 8 * slot), x)
        for part, y in zip(parts, x.parts, strict=True):
            pending.append((pn, (n, part), y))

    corners = ((lo, beyond), (lo, pl.ds(3 * H + B, H)), (pl.ds(H, H), pl.ds(2 * H + B, H)))
    for n, slot in ((0, 3), (3, 0), (4, 1), (5, 2), (1, 0), (2, 1)):
        landed = corners[2] if n in (1, 2) else corners[1]
        pack_e, pack_w = (Batch(pack[part] for part in landed) for pack in (pe, pw))
        spread(n, corners[0], pack_e, pack_w, slot, edges(FIELDS[n], corners[0]))
    landed = [pl.ds(i * 8 + 2 * H, 8) for i in range(B // 8)]
    pack_e, pack_w = (Batch(pack[part] for part in landed) for pack in (pe, pw))
    for n, slot in ((0, 3), (3, 0), (4, 1), (5, 2)):
        spread(n, held_blocks, pack_e, pack_w, slot, read(pn, n))
    from_spare_e = jnp.where(place < 12, lane - 4, lane + 2)
    from_spare_w = jnp.where(place < 20, lane - 18, lane - 12)
    from_spare = jnp.where(place < 16, from_spare_e, from_spare_w) % B
    x = where(far_hi, picked(pack_e, from_spare), read(pn, 2))
    far_v = where(far_lo, picked(pack_w, from_spare), x)
    write(pn, (2,), far_v)
    flush(pending)
    run_hi = (place >= 9) & (place < 14)
    run_lo = (place >= 17) & (place < 23)
    own = read(pn, 1)
    dv = far_v - Batch(pn[2, pl.ds(i * 8 + H - 1, 8)] for i in range(B // 8))
    x = where(run_hi, where(place == 9, own, -dv), 0.0)
    y = where(run_lo, where(place == 22, own, rolled(dv, -1)), 0.0)
    x2, y2 = x + rolled(x, 1), y + rolled(y, -1)
    x, y = x2 + rolled(x2, 2) + rolled(x, 4), y2 + rolled(y2, -2) + rolled(y2, -4)
    write(pn, (1,), where(far_hi, x, where(far_lo, y, own)))
    flush(pending)
    for r in range(R):
        for n in range(len(FIELDS)):
            keep(n, K, r, pn[n, pl.ds(r, 8, stride=R)])
        flush(pending)

    flat = ext.reshape(32 * E, B)
    for r in range(S):
        for n, field in enumerate(FIELDS):
            south_rows = flat[pl.ds(field * E + H - 6 + r, 8, stride=E), :]
            north_rows = flat[pl.ds((field - K) * E + H + 120 + r, 8, stride=E), :]
            keep(n, K + 1, r, jnp.where(sub < 4, south_rows, north_rows))
        flush(pending)

    for r in (6, 7, 10, 11):
        for n in range(3):
            levels(n, r)
        flush(pending)
    prepare(K, range(R), R, bend, last, True)
    prepare(K + 1, range(S), S, 7, last_strip, False)
    lax.fori_loop(0, K, functools.partial(prepare_level, range(6, 11)), 0)

    def advect_edges(i, carry):
        advect(K, R, bend)
        advect(K + 1, S, 7)
        return carry

    lax.fori_loop(0, 2, advect_edges, 0)

    def merged(x, edge, k, low, high):
        source = jnp.where(lane < B // 2, lane + 32 * k + 22, lane + 32 * k + 10) % B
        return where((lane < low) | (lane >= high), picked(edge, source), x)

    ends = (sub == 0) | (sub == 7)
    for t in range(T):
        for k in range(K):
            source = jnp.where(sub == 0, k, 4 + k)
            x = [tr[t, k, r] for r in range(R)]
            for r in range(6, 12):
                x[r] = jnp.where(ends, jnp.take_along_axis(tr[t, K + 1, r - 2], source, axis=0), x[r])
            x = merged(Batch(x), Batch(tr[t, K, r] for r in range(R)), k, 4, B - 4)
            for r in range(R):
                pending.append((tr, (t, k, r), x.parts[r]))
            flush(pending)

    lax.fori_loop(0, K + 1, advect_level, 0)

    for start in range(0, R, 6):
        strided = [pl.ds(r, 8, stride=R) for r in range(start, start + 6)]

        def rows_of(ref, *index):
            return Batch(ref[(*index, r)] for r in range(start, start + 6))

        def both(ref, first, k, low, high):
            return merged(rows_of(ref, *first, k), rows_of(ref, *first, K), k, low, high)

        def leave(first, solved):
            for k in range(K):
                for part, x in zip(strided, solved[k].parts, strict=True):
                    pending.append((res, (first + k, part), x))

        mix = [Batch(dext[k, part] for part in strided) for k in range(K - 1)]
        gu = [both(cx, (0,), k, 0, B - 1) for k in range(K)]
        un = [both(new, (0,), k, 1, B - 1) for k in range(K)]
        (un,) = solve([un], [mix[k] * (gu[k] * gu[k + 1]) for k in range(K - 1)])
        leave(0, un)
        gv = [rows_of(cy, 0, k) for k in range(K)]
        vn = [both(new, (1,), k, 1, B - 1) for k in range(K)]
        (vn,) = solve([vn], [mix[k] * (gv[k] * gv[k + 1]) for k in range(K - 1)])
        leave(K, vn)
        w = [rows_of(wet, k) for k in range(K)]
        mix = [mix[k] * (w[k] * w[k + 1]) for k in range(K - 1)]
        x = [[both(tr, (t,), k, 2, B - 2) for k in range(K)] for t in range(T)]
        for t, solved in enumerate(solve(x, mix)):
            leave(2 * K + t * K, solved)
        flush(pending)


def stepped(nlat, nlon, u, v, q, m, d):
    hbm = pl.BlockSpec(memory_space=pltpu.HBM)
    return pl.pallas_call(
        functools.partial(step, nlat, nlon),
        out_shape=jax.ShapeDtypeStruct(((2 + T) * K, E, B), F32),
        in_specs=[hbm] * 5,
        out_specs=pl.BlockSpec(memory_space=pltpu.VMEM),
        scratch_shapes=[
            pltpu.VMEM((32, E, B), F32),
            pltpu.VMEM((K, B, B), jnp.int32),
            pltpu.VMEM((K - 1, E, B), F32),
            pltpu.VMEM(((2 + T) * K, H, B), F32),
            pltpu.VMEM(((2 + T) * K, H, B), F32),
            pltpu.VMEM((K, H, B), jnp.int32),
            pltpu.VMEM((K, H, B), jnp.int32),
            pltpu.VMEM((B + 4 * H, B), F32),
            pltpu.VMEM((B + 4 * H, B), F32),
            pltpu.VMEM((E, B), F32),
            pltpu.VMEM((E, B), F32),
            pltpu.VMEM((len(FIELDS), E, B), F32),
            pltpu.VMEM((2, K + 2, R, 8, B), F32),
            pltpu.VMEM((2, K + 1, R, 8, B), F32),
            pltpu.VMEM((T, K + 2, R, 8, B), F32),
            pltpu.VMEM((K + 2, R, 8, B), F32),
            pltpu.VMEM((6, K + 2, R, 8, B), F32),
            pltpu.VMEM((3, K + 2, R, 8, B), F32),
            pltpu.VMEM((2, K + 2, 8, B), F32),
            pltpu.VMEM((2, R, 8, B), F32),
            pltpu.SemaphoreType.DMA((7,)),
            pltpu.SemaphoreType.DMA((14,)),
            pltpu.SemaphoreType.DMA((14,)),
        ],
        compiler_params=pltpu.CompilerParams(
            collective_id=0, has_side_effects=True, vmem_limit_bytes=40 * 2**20
        ),
    )(u, v, q, m, d)


def deliver(res, u, v, q, done):
    middle = pl.ds(H, B)
    copies = [
        pltpu.make_async_copy(res.at[0:K, middle], u, done.at[0]),
        pltpu.make_async_copy(res.at[K : 2 * K, middle], v, done.at[1]),
        pltpu.make_async_copy(res.at[2 * K :, middle], q, done.at[2]),
    ]
    for copy in copies:
        copy.start()
    for copy in copies:
        copy.wait()


def delivered(res):
    return pl.pallas_call(
        deliver,
        out_shape=(
            jax.ShapeDtypeStruct((K, B, B), F32),
            jax.ShapeDtypeStruct((K, B, B), F32),
            jax.ShapeDtypeStruct((T * K, B, B), F32),
        ),
        in_specs=[pl.BlockSpec(memory_space=pltpu.VMEM)],
        out_specs=[pl.BlockSpec(memory_space=pltpu.HBM)] * 3,
        scratch_shapes=[pltpu.SemaphoreType.DMA((3,))],
    )(res)


def per_device(nlat, nlon, zonal_flow, meridional_flow, tracers, sea_mask, diffusivity):
    q = tracers.reshape(T * K, B, B)
    given = [
        pltpu.with_memory_space_constraint(x, pltpu.HBM)
        for x in (zonal_flow, meridional_flow, q, sea_mask, diffusivity)
    ]
    res = pltpu.with_memory_space_constraint(stepped(nlat, nlon, *given), pltpu.VMEM)
    u, v, q = delivered(res)
    return u, v, q.reshape(T, K, B, B)


def solution(mesh):
    cells = P(None, "lat", "lon")
    traced = P(None, None, "lat", "lon")
    return jax.shard_map(
        functools.partial(per_device, mesh.shape["lat"], mesh.shape["lon"]),
        mesh=mesh,
        in_specs=(cells, cells, traced, cells, cells),
        out_specs=(cells, cells, traced),
        check_vma=False,
    )
```

```python
import functools
import math

import jax
import jax.numpy as jnp
from jax import lax
from jax.experimental import pallas as pl
from jax.experimental.pallas import tpu as pltpu
from jax.sharding import PartitionSpec as P

K = 4
T = 3
NSUB = 3
B = 128
H = 8
E = B + 2 * H
R = E // 8
S = 14
DEPTH = R
WET, U, V, Q = 4, 8, 12, 16
FIELDS = (WET, U, V, Q, Q + K, Q + 2 * K)
DEPTHS = [(f, 4 if U <= f < V else 5 if V <= f < Q else 6) for f in range(WET, Q + T * K)]
ROWS = [(f, n, sum(m for _, m in DEPTHS[:i])) for i, (f, n) in enumerate(DEPTHS)]
SENT = -(-sum(n for _, n in DEPTHS) // 8) * 8
F32 = jnp.float32
MESH = pl.DeviceIdType.MESH
coriolis_peak = 0.5


def flush(pending):
    for ref, index, x in pending:
        ref[index] = x
    pending.clear()


class Batch:
    def __init__(self, parts):
        self.parts = list(parts)

    def __add__(self, other):
        return each(jnp.add, self, other)

    __radd__ = __add__

    def __sub__(self, other):
        return each(jnp.subtract, self, other)

    def __rsub__(self, other):
        return each(jnp.subtract, other, self)

    def __mul__(self, other):
        return each(jnp.multiply, self, other)

    __rmul__ = __mul__

    def __rtruediv__(self, other):
        return each(jnp.divide, other, self)

    def __neg__(self):
        return each(jnp.negative, self)

    def __gt__(self, other):
        return each(jnp.greater, self, other)


def each(function, *given):
    size = [len(x.parts) for x in given if isinstance(x, Batch)]
    if not size:
        return function(*given)
    return Batch(
        function(*(x.parts[n] if isinstance(x, Batch) else x for x in given)) for n in range(size[0])
    )


def where(mask, a, b):
    return each(jnp.where, mask, a, b)


def minmod(a, b):
    return each(jnp.maximum, each(jnp.minimum, a, b), each(jnp.minimum, each(jnp.maximum, a, b), 0.0))


def following(x):
    return each(lambda part: pltpu.roll(part, B - 1, 1), x)


def preceding(x):
    return each(lambda part: pltpu.roll(part, 1, 1), x)


def above(x):
    return pltpu.roll(x, 7, 0)


def below(x):
    return pltpu.roll(x, 1, 0)


def rolled(x, amount):
    return each(lambda part: pltpu.roll(part, amount % B, 1), x) if amount % B else x


def picked(x, index):
    return each(lambda part: jnp.take_along_axis(part, index, axis=1), x)


def flipped(x, index):
    x = jnp.take_along_axis(x, index, axis=1)
    backward = 7 - lax.broadcasted_iota(jnp.int32, (8, B), 0)
    return jnp.take_along_axis(x, backward, axis=0)


def solve(x, coupling):
    carried = []
    inverse = []
    for k in range(K):
        divisor = 1.0
        if k < K - 1:
            divisor = divisor + coupling[k]
        if k > 0:
            divisor = divisor + coupling[k - 1] * (1.0 - carried[k - 1])
        inverse.append(1.0 / divisor)
        if k < K - 1:
            carried.append(coupling[k] * inverse[k])
    results = []
    for field in x:
        scaled = [field[0] * inverse[0]]
        for k in range(1, K):
            scaled.append((field[k] + coupling[k - 1] * scaled[k - 1]) * inverse[k])
        solved = [scaled[K - 1]]
        for k in range(K - 2, -1, -1):
            solved.insert(0, scaled[k] + carried[k] * solved[0])
        results.append(solved)
    return results


def step(
    nlat, nlon, u, v, q, m, d, res,
    ext, mext, dext, hn, hs, pe, pw, kn, ks, ke, kw, pn, flow, new, tr, wet, cx, cy, fold, cor, load, send, recv,
):
    lat = lax.axis_index("lat")
    lon = lax.axis_index("lon")
    top = lat == nlat - 1
    bottom = lat == 0
    east = lax.rem(lon + 1, nlon)
    west = lax.rem(lon + nlon - 1, nlon)
    n_lat = jnp.where(top, lat, lat + 1)
    n_mid = jnp.where(top, nlon - 1 - lon, lon)
    n_west = jnp.where(top, lax.rem(nlon - lon, nlon), west)
    n_east = jnp.where(top, lax.rem(2 * nlon - 2 - lon, nlon), east)
    s_lat = jnp.maximum(lat - 1, 0)
    own_w = n_west == lon
    own_e = n_east == lon

    def at(row, column):
        return {"lat": row, "lon": column}

    middle = pl.ds(H, B)
    beyond = pl.ds(H + B, H)
    loads = [
        pltpu.make_async_copy(u, ext.at[U : U + K, middle], load.at[0]),
        pltpu.make_async_copy(v, ext.at[V : V + K, middle], load.at[1]),
        pltpu.make_async_copy(q, ext.at[Q : Q + T * K, middle], load.at[2]),
        pltpu.make_async_copy(m, mext, load.at[3]),
        pltpu.make_async_copy(d, dext.at[:, middle], load.at[4]),
    ]
    for copy in loads:
        copy.start()

    barrier = pltpu.get_barrier_semaphore()

    def greet(row, column):
        pl.semaphore_signal(barrier, inc=1, device_id=at(row, column), device_id_type=MESH)

    greet(lat, east)
    greet(lat, west)
    greet(n_lat, n_mid)

    @pl.when(jnp.logical_not(top & own_w))
    def _():
        greet(n_lat, n_west)

    @pl.when(jnp.logical_not(top & own_e))
    def _():
        greet(n_lat, n_east)

    @pl.when(jnp.logical_not(bottom))
    def _():
        greet(s_lat, lon)
        greet(s_lat, west)
        greet(s_lat, east)

    def remote(src, dst, slot, row, column):
        return pltpu.make_async_remote_copy(
            src_ref=src,
            dst_ref=dst,
            send_sem=send.at[slot],
            recv_sem=recv.at[slot],
            device_id=at(row, column),
            device_id_type=MESH,
        )

    lo = pl.ds(0, H)
    lo_held = pl.ds(H, H)
    hi_held = pl.ds(B, H)

    sent, arrived = pl.ds(0, SENT), pl.ds(H, SENT)
    to_north = [remote(kn.at[sent], hs.at[arrived], 5, n_lat, n_mid)]
    over_fold = [remote(kn.at[sent], hn.at[arrived], 2, n_lat, n_mid)]
    to_south = [remote(ks.at[sent], hn.at[arrived], 2, s_lat, lon)]

    own_rows, lo_pack, hi_pack = pl.ds(H, B), pl.ds(0, 2 * H), pl.ds(B, 2 * H)
    lo_land, mid_land, hi_land = pl.ds(0, 2 * H), pl.ds(2 * H, B), pl.ds(2 * H + B, 2 * H)
    sends = [
        remote(ke.at[own_rows], pw.at[mid_land], 1, lat, east),
        remote(kw.at[own_rows], pe.at[mid_land], 0, lat, west),
    ]
    north_east = remote(ke.at[hi_pack], pw.at[lo_land], 7, n_lat, n_east)
    north_west = remote(kw.at[hi_pack], pe.at[lo_land], 6, n_lat, n_west)
    fold_west = remote(kw.at[hi_pack], pw.at[hi_land], 4, n_lat, n_west)
    fold_east = remote(ke.at[hi_pack], pe.at[hi_land], 3, n_lat, n_east)
    self_west = pltpu.make_async_copy(kw.at[hi_pack], pw.at[hi_land], load.at[5])
    self_east = pltpu.make_async_copy(ke.at[hi_pack], pe.at[hi_land], load.at[6])
    south_east = remote(ke.at[lo_pack], pw.at[hi_land], 4, s_lat, east)
    south_west = remote(kw.at[lo_pack], pe.at[hi_land], 3, s_lat, west)

    def enter():
        peers = (
            3
            + jnp.where(top & own_w, 0, 1)
            + jnp.where(top & own_e, 0, 1)
            + jnp.where(bottom, 0, 3)
        )
        pl.semaphore_wait(barrier, peers)

        @pl.when(jnp.logical_not(top))
        def _():
            north_east.start()
            north_west.start()

        @pl.when(top & own_w)
        def _():
            self_west.start()

        @pl.when(top & jnp.logical_not(own_w))
        def _():
            fold_west.start()

        @pl.when(top & own_e)
        def _():
            self_east.start()

        @pl.when(top & jnp.logical_not(own_e))
        def _():
            fold_east.start()

        @pl.when(jnp.logical_not(bottom))
        def _():
            south_east.start()
            south_west.start()

        @pl.when(top)
        def _():
            for copy in over_fold:
                copy.start()

        @pl.when(jnp.logical_not(top))
        def _():
            for copy in to_north:
                copy.start()

        @pl.when(jnp.logical_not(bottom))
        def _():
            for copy in to_south:
                copy.start()

    lane = lax.broadcasted_iota(jnp.int32, (8, B), 1)
    sub = lax.broadcasted_iota(jnp.int32, (8, B), 0)
    group = lane // 8

    reached_late = lon >= nlon // 2

    for f in range(WET, Q + T * K):
        ext[f, lo] = jnp.zeros((H, B), F32)
        ext[f, beyond] = jnp.zeros((H, B), F32)
    for landing in (hn, hs):
        landing[lo] = jnp.zeros((H, B), F32)
        landing[pl.ds(H + SENT, H)] = jnp.zeros((H, B), F32)
    for copy in loads:
        copy.wait()

    place = lane % 32
    level = lane // 32
    spare_w = (place == 6) | (place == 7) | (place == 14) | (place == 15)
    spare_e = (place == 0) | (place == 1) | (place == 8) | (place == 9)
    spare_of = jnp.where(
        spare_w,
        jnp.where(place < 8, place - 6, place - 12),
        jnp.where(place < 8, B - 4 + place, B - 10 + place),
    )
    spare_of = jnp.minimum(spare_of, B - 1)

    held_blocks = [pl.ds(i * 8 + H, 8) for i in range(B // 8)]
    inner_blocks = held_blocks[1:-1]
    outer_blocks = [lo_held, hi_held]

    def read(ref, *index, parts=held_blocks):
        return Batch(ref[(*index, part)] for part in parts)

    pending = []

    def write(ref, index, x, parts=held_blocks):
        for part, y in zip(parts, x.parts, strict=True):
            pending.append((ref, (*index, part), y))

    for k in range(K):
        sea = Batch(mext[k, pl.ds(i * 8, 8)].astype(F32) for i in range(B // 8))
        write(ext, (WET + k,), sea)
    flush(pending)

    def pack(parts):
        packed_w = packed_e = Batch([jnp.zeros((8, B), F32)] * len(parts))
        for k in range(K):
            for f, field in enumerate((Q, Q + K, Q + 2 * K, WET)):
                j = 4 * k + f
                x = rolled(read(ext, field + k, parts=parts), 8 * j)
                packed_w = where(group == j, x, packed_w)
                packed_e = where(group == (j - 1) % 16, x, packed_e)
            x = picked(read(ext, V + k, parts=parts), spare_of)
            packed_w = where(spare_w & (level == k), x, packed_w)
            packed_e = where(spare_e & (level == k), x, packed_e)
        write(kw, (), packed_w, parts)
        write(ke, (), packed_e, parts)

    def pack_flow(parts, into):
        packed_w = packed_e = Batch([jnp.zeros((8, B), F32)] * len(parts))
        for k in range(K):
            for f, field in enumerate((U, V)):
                j = 4 * k + f
                x = rolled(read(ext, field + k, parts=parts), 8 * j)
                packed_w = where(group == j, x, packed_w)
                packed_e = where(group == (j - 1) % 16, x, packed_e)
        write(kw, (), packed_w, into)
        write(ke, (), packed_e, into)

    pack(outer_blocks)
    pack_flow(outer_blocks, [lo, beyond])
    flush(pending)
    for f, n, at in ROWS:
        kn[pl.ds(at, 8)] = ext[f, pl.ds(H + B - n, 8)]
        ks[pl.ds(at, 8)] = ext[f, lo_held]

    @pl.when(reached_late)
    def _():
        enter()

    pack(inner_blocks)
    flush(pending)

    @pl.when(reached_late)
    def _():
        for copy in sends:
            copy.start()

    far_hi = (place >= 10) & (place < 16)
    far_lo = (place >= 16) & (place < 22)
    source_of = (place + jnp.where(place < 16, 118, B - 22)) % B

    def edges(field, parts):
        edge = picked(Batch(ext[field, part] for part in parts), source_of)
        for k in range(1, K):
            x = picked(Batch(ext[field + k, part] for part in parts), source_of)
            edge = where(level == k, x, edge)
        return edge

    for n, field in enumerate(FIELDS):
        write(pn, (n,), edges(field, held_blocks))
        flush(pending)

    def keep(n, i, r, x):
        ref, index = (wet, (i, r)) if n == 0 else (flow, (n - 1, i, r)) if n < 3 else (tr, (n - 3, i, r))
        pending.append((ref, index, x))

    def levels(n, r):
        for k in range(K):
            keep(n, k, r, ext[FIELDS[n] + k, pl.ds(r, 8, stride=R)])

    for r in range(R):
        for n in range(len(FIELDS)):
            levels(n, r)
        flush(pending)

    @pl.when(jnp.logical_not(reached_late))
    def _():
        enter()
        for copy in sends:
            copy.start()

    def coriolis(offset):
        row = lat * B + R * sub + lane - H
        ny = nlat * B
        return coriolis_peak * jnp.sin(math.pi * ((row.astype(F32) + offset) / ny - 0.5))

    for f, offset in enumerate((0.5, 1.0)):
        turning = coriolis(offset)
        for r in range(R):
            cor[f, r] = jnp.broadcast_to(turning[:, r : r + 1], (8, B))

    def prepare(i, rows, count, bend, beyond_fold, momentum):
        def get(f, r):
            if r == -1:
                return below(flow[f, i, count - 1])
            if r == count:
                return above(flow[f, i, 0])
            return flow[f, i, r]

        for start in range(0, len(rows), 9):
            chunk = rows[start : start + 9]

            def put(ref, index, x):
                for r, y in zip(chunk, x.parts, strict=True):
                    held_back.append((ref, (index, i, r), y))

            def bent(a, b):
                return Batch(
                    jnp.where(beyond_fold, x, y) if r > bend else y
                    for r, x, y in zip(chunk, a.parts, b.parts, strict=True)
                )

            held_back = []
            u0, v0 = (Batch(get(f, r) for r in chunk) for f in range(2))
            un, vn = (Batch(get(f, r + 1) for r in chunk) for f in range(2))
            w0 = Batch(wet[i, r] for r in chunk)
            wn = Batch(wet[i, r + 1] if r < count - 1 else above(wet[i, 0]) for r in chunk)
            gu = w0 * following(w0)
            gv = w0 * wn
            ue = following(u0)
            uw = preceding(u0)
            gw = preceding(gu)
            ua = bent(ue, u0)
            wa = bent(u0, uw)
            va = bent(vn, v0)
            put(cx, 0, gu)
            put(cx, 1, each(jnp.maximum, ua, 0.0) * gu)
            put(cx, 2, 0.5 - 0.5 * ua)
            put(cx, 3, gw)
            put(cx, 4, each(jnp.minimum, wa, 0.0) * gw)
            put(cx, 5, -0.5 - 0.5 * wa)
            put(cy, 0, gv)
            put(cy, 1, va * gv)
            put(cy, 2, where(va > 0.0, 0.5, -0.5) - 0.5 * va)
            if bend in chunk:
                n = chunk.index(bend)
                vf = jnp.where(beyond_fold, vn.parts[n], v0.parts[n])
                held_back.append((fold, (0, i), vf * gv.parts[n]))
                held_back.append((fold, (1, i), jnp.where(vf > 0.0, 0.5, -0.5) - 0.5 * vf))
            if momentum:
                us, vs = (Batch(get(f, r - 1) for r in chunk) for f in range(2))
                turn_u, turn_v = (Batch(cor[f, r] for r in chunk) for f in range(2))
                a = v0 + vs
                vbar = 0.25 * (a + following(a))
                a = u0 + un
                ubar = 0.25 * (a + preceding(a))
                du = vbar * (turn_u - 0.5 * (un - us)) - 0.5 * u0 * (ue - uw)
                dv = -ubar * (turn_v + 0.5 * (following(v0) - preceding(v0))) - 0.5 * v0 * (vn - vs)
                put(new, 0, u0 + gu * du)
                put(new, 1, v0 + gv * dv)
            flush(held_back)

    last = top & (sub == 7)
    last_strip = top & (sub >= 4)
    bend = R - H - 1

    def prepare_level(rows, i, carry):
        prepare(i, rows, R, bend, last, True)
        return carry

    lax.fori_loop(0, K, functools.partial(prepare_level, range(R)), 0)

    def face(w, c, here, there, slope_here, slope_there):
        way = w > 0.0
        return w * (jnp.where(way, here, there) + c * jnp.where(way, slope_here, slope_there))

    def advect(i, count, bend):
        first, held_back = [None] * T, []
        turned, last_jump, last_slope = [], [], []
        now, ahead, jump, slope, south = [], [], [], [], []
        for t in range(T):
            x0, x1 = tr[t, i, 0], tr[t, i, 1]
            xr = above(x0)
            jr = (xr - tr[t, i, count - 1]) * cy[0, i, count - 1]
            j0 = (x1 - x0) * cy[0, i, 0]
            s0 = minmod(j0, below(jr))
            turned.append(xr)
            last_jump.append(jr)
            last_slope.append(above(s0))
            now.append(x0)
            ahead.append(x1)
            jump.append(j0)
            slope.append(s0)
            south.append(None)
        state = {}

        def stage_a(t, r):
            x = tr[t, i, r]
            state[t, r] = (following(x), preceding(x))

        def stage_b(t, r):
            e, p = state[t, r]
            x = tr[t, i, r]
            s = minmod((e - x) * cx[0, i, r], (x - p) * cx[3, i, r])
            a = cx[1, i, r] * (x + cx[2, i, r] * s)
            b = cx[4, i, r] * (x + cx[5, i, r] * s)
            state[t, r] = (b - a, preceding(a), following(b))

        def stage_e(t, r):
            own, a, b = state.pop((t, r))
            x, xn = now[t], ahead[t]
            if r + 1 < count - 1:
                xnn = tr[t, i, r + 2]
                jn = (xnn - xn) * cy[0, i, r + 1]
                sn = minmod(jn, jump[t])
            elif r + 1 == count - 1:
                xnn = turned[t]
                jn = last_jump[t]
                sn = minmod(jn, jump[t])
            else:
                xnn = jn = None
                sn = last_slope[t]
            north = face(cy[1, i, r], cy[2, i, r], x, xn, slope[t], sn)
            y = x - north if r == 0 else x - (north - south[t])
            if r == bend:
                north = face(fold[0, i], fold[1, i], x, xn, slope[t], sn)
            south[t] = north
            now[t], ahead[t], jump[t], slope[t] = xn, xnn, jn, sn
            y = y + (own + (a - b))
            if r == 0:
                first[t] = y
            else:
                held_back.append((tr, (t, i, r), y))

        stages = [stage_a, stage_b, stage_e]
        for tick in range(count + 2 * DEPTH):
            for n in (2, 1, 0):
                r = tick - n * DEPTH
                if 0 <= r < count:
                    for t in range(T):
                        stages[n](t, r)
            if tick % 3 == 2:
                flush(held_back)
        flush(held_back)
        for t in range(T):
            tr[t, i, 0] = first[t] + below(south[t])

    def advect_level(i, carry):
        advect(lax.rem(i, K + 1), R, bend)
        return carry

    def advect_inner(i, carry):
        advect(lax.rem(i, K), R, bend)
        return carry

    lax.fori_loop(0, 2 * K, advect_inner, 0)

    for copy in sends:
        copy.wait_send()

    @pl.when(top)
    def _():
        for copy in over_fold:
            copy.wait_send()

    @pl.when(jnp.logical_not(top))
    def _():
        for copy in to_north:
            copy.wait_send()
        north_east.wait_send()
        north_west.wait_send()

    @pl.when(top & own_w)
    def _():
        self_west.wait()

    @pl.when(top & jnp.logical_not(own_w))
    def _():
        fold_west.wait_send()

    @pl.when(top & own_e)
    def _():
        self_east.wait()

    @pl.when(top & jnp.logical_not(own_e))
    def _():
        fold_east.wait_send()

    @pl.when(jnp.logical_not(bottom))
    def _():
        for copy in to_south:
            copy.wait_send()
        south_east.wait_send()
        south_west.wait_send()

    for copy in sends:
        copy.wait_recv()
    for copy in to_south:
        copy.wait_recv()

    @pl.when(jnp.logical_not(top & own_w))
    def _():
        south_east.wait_recv()

    @pl.when(jnp.logical_not(top & own_e))
    def _():
        south_west.wait_recv()

    @pl.when(jnp.logical_not(bottom))
    def _():
        for copy in to_north:
            copy.wait_recv()
        north_east.wait_recv()
        north_west.wait_recv()


    for f, n, at in ROWS:
        pending.append((ext, (f, lo), hs[pl.ds(at + n, 8)]))
        pending.append((ext, (f, beyond), hn[pl.ds(at + H, 8)]))
    flush(pending)

    @pl.when(bottom)
    def _():
        for f in range(WET, Q + T * K):
            ext[f, lo] = jnp.zeros((H, B), F32)
        pe[lo_land] = jnp.zeros((2 * H, B), F32)
        pw[lo_land] = jnp.zeros((2 * H, B), F32)

    @pl.when(top)
    def _():
        whole = B - 1 - lane
        turned = [flipped(hn[pl.ds(at + n, 8)], whole) for _, n, at in ROWS]
        for f, x in enumerate(turned, WET):
            ext[f, beyond] = -x if U <= f < Q else x
        within = 7 - lane % 8
        from_east = (lane // 8 + 15) % 16 * 8 + within
        from_west = (lane // 8 + 1) % 16 * 8 + within
        first, second = pl.ds(2 * H + B, H), pl.ds(3 * H + B, H)
        for landed, source in ((pe, from_east), (pw, from_west)):
            x, y = flipped(landed[first], source), flipped(landed[second], source)
            landed[first] = -y
            landed[second] = x

    def spread(n, parts, pack_e, pack_w, slot, own):
        x = where(far_hi, rolled(pack_e, 10 - 8 * slot), own)
        x = where(far_lo, rolled(pack_w, 22 - 8 * slot), x)
        for part, y in zip(parts, x.parts, strict=True):
            pending.append((pn, (n, part), y))

    corners = ((lo, beyond), (lo, pl.ds(3 * H + B, H)), (pl.ds(H, H), pl.ds(2 * H + B, H)))
    for n, slot in ((0, 3), (3, 0), (4, 1), (5, 2), (1, 0), (2, 1)):
        landed = corners[2] if n in (1, 2) else corners[1]
        pack_e, pack_w = (Batch(pack[part] for part in landed) for pack in (pe, pw))
        spread(n, corners[0], pack_e, pack_w, slot, edges(FIELDS[n], corners[0]))
    landed = [pl.ds(i * 8 + 2 * H, 8) for i in range(B // 8)]
    pack_e, pack_w = (Batch(pack[part] for part in landed) for pack in (pe, pw))
    for n, slot in ((0, 3), (3, 0), (4, 1), (5, 2)):
        spread(n, held_blocks, pack_e, pack_w, slot, read(pn, n))
    from_spare_e = jnp.where(place < 12, lane - 4, lane + 2)
    from_spare_w = jnp.where(place < 20, lane - 18, lane - 12)
    from_spare = jnp.where(place < 16, from_spare_e, from_spare_w) % B
    x = where(far_hi, picked(pack_e, from_spare), read(pn, 2))
    far_v = where(far_lo, picked(pack_w, from_spare), x)
    write(pn, (2,), far_v)
    flush(pending)
    run_hi = (place >= 9) & (place < 14)
    run_lo = (place >= 17) & (place < 23)
    own = read(pn, 1)
    dv = far_v - Batch(pn[2, pl.ds(i * 8 + H - 1, 8)] for i in range(B // 8))
    x = where(run_hi, where(place == 9, own, -dv), 0.0)
    y = where(run_lo, where(place == 22, own, rolled(dv, -1)), 0.0)
    x2, y2 = x + rolled(x, 1), y + rolled(y, -1)
    x, y = x2 + rolled(x2, 2) + rolled(x, 4), y2 + rolled(y2, -2) + rolled(y2, -4)
    write(pn, (1,), where(far_hi, x, where(far_lo, y, own)))
    flush(pending)
    for r in range(R):
        for n in range(len(FIELDS)):
            keep(n, K, r, pn[n, pl.ds(r, 8, stride=R)])
        flush(pending)

    flat = ext.reshape(32 * E, B)
    for r in range(S):
        for n, field in enumerate(FIELDS):
            south_rows = flat[pl.ds(field * E + H - 6 + r, 8, stride=E), :]
            north_rows = flat[pl.ds((field - K) * E + H + 120 + r, 8, stride=E), :]
            keep(n, K + 1, r, jnp.where(sub < 4, south_rows, north_rows))
        flush(pending)

    for r in (6, 7, 10, 11):
        for n in range(3):
            levels(n, r)
        flush(pending)
    prepare(K, range(R), R, bend, last, True)
    prepare(K + 1, range(S), S, 7, last_strip, False)
    lax.fori_loop(0, K, functools.partial(prepare_level, range(6, 11)), 0)

    def advect_edges(i, carry):
        advect(K, R, bend)
        advect(K + 1, S, 7)
        return carry

    lax.fori_loop(0, 2, advect_edges, 0)

    def merged(x, edge, k, low, high):
        source = jnp.where(lane < B // 2, lane + 32 * k + 22, lane + 32 * k + 10) % B
        return where((lane < low) | (lane >= high), picked(edge, source), x)

    ends = (sub == 0) | (sub == 7)
    for t in range(T):
        for k in range(K):
            source = jnp.where(sub == 0, k, 4 + k)
            x = [tr[t, k, r] for r in range(R)]
            for r in range(6, 12):
                x[r] = jnp.where(ends, jnp.take_along_axis(tr[t, K + 1, r - 2], source, axis=0), x[r])
            x = merged(Batch(x), Batch(tr[t, K, r] for r in range(R)), k, 4, B - 4)
            for r in range(R):
                pending.append((tr, (t, k, r), x.parts[r]))
            flush(pending)

    lax.fori_loop(0, K + 1, advect_level, 0)

    for start in range(0, R, 6):
        strided = [pl.ds(r, 8, stride=R) for r in range(start, start + 6)]

        def rows_of(ref, *index):
            return Batch(ref[(*index, r)] for r in range(start, start + 6))

        def both(ref, first, k, low, high):
            return merged(rows_of(ref, *first, k), rows_of(ref, *first, K), k, low, high)

        def leave(first, solved):
            for k in range(K):
                for part, x in zip(strided, solved[k].parts, strict=True):
                    pending.append((res, (first + k, part), x))

        mix = [Batch(dext[k, part] for part in strided) for k in range(K - 1)]
        gu = [both(cx, (0,), k, 0, B - 1) for k in range(K)]
        un = [both(new, (0,), k, 1, B - 1) for k in range(K)]
        (un,) = solve([un], [mix[k] * (gu[k] * gu[k + 1]) for k in range(K - 1)])
        leave(0, un)
        gv = [rows_of(cy, 0, k) for k in range(K)]
        vn = [both(new, (1,), k, 1, B - 1) for k in range(K)]
        (vn,) = solve([vn], [mix[k] * (gv[k] * gv[k + 1]) for k in range(K - 1)])
        leave(K, vn)
        w = [rows_of(wet, k) for k in range(K)]
        mix = [mix[k] * (w[k] * w[k + 1]) for k in range(K - 1)]
        x = [[both(tr, (t,), k, 2, B - 2) for k in range(K)] for t in range(T)]
        for t, solved in enumerate(solve(x, mix)):
            leave(2 * K + t * K, solved)
        flush(pending)


def stepped(nlat, nlon, u, v, q, m, d):
    hbm = pl.BlockSpec(memory_space=pltpu.HBM)
    return pl.pallas_call(
        functools.partial(step, nlat, nlon),
        out_shape=jax.ShapeDtypeStruct(((2 + T) * K, E, B), F32),
        in_specs=[hbm] * 5,
        out_specs=pl.BlockSpec(memory_space=pltpu.VMEM),
        scratch_shapes=[
            pltpu.VMEM((32, E, B), F32),
            pltpu.VMEM((K, B, B), jnp.int32),
            pltpu.VMEM((K - 1, E, B), F32),
            pltpu.VMEM((SENT + 2 * H, B), F32),
            pltpu.VMEM((SENT + 2 * H, B), F32),
            pltpu.VMEM((B + 4 * H, B), F32),
            pltpu.VMEM((B + 4 * H, B), F32),
            pltpu.VMEM((SENT + H, B), F32),
            pltpu.VMEM((SENT + H, B), F32),
            pltpu.VMEM((E, B), F32),
            pltpu.VMEM((E, B), F32),
            pltpu.VMEM((len(FIELDS), E, B), F32),
            pltpu.VMEM((2, K + 2, R, 8, B), F32),
            pltpu.VMEM((2, K + 1, R, 8, B), F32),
            pltpu.VMEM((T, K + 2, R, 8, B), F32),
            pltpu.VMEM((K + 2, R, 8, B), F32),
            pltpu.VMEM((6, K + 2, R, 8, B), F32),
            pltpu.VMEM((3, K + 2, R, 8, B), F32),
            pltpu.VMEM((2, K + 2, 8, B), F32),
            pltpu.VMEM((2, R, 8, B), F32),
            pltpu.SemaphoreType.DMA((7,)),
            pltpu.SemaphoreType.DMA((8,)),
            pltpu.SemaphoreType.DMA((8,)),
        ],
        compiler_params=pltpu.CompilerParams(
            collective_id=0, has_side_effects=True, vmem_limit_bytes=40 * 2**20
        ),
    )(u, v, q, m, d)


def deliver(res, u, v, q, done):
    middle = pl.ds(H, B)
    copies = [
        pltpu.make_async_copy(res.at[0:K, middle], u, done.at[0]),
        pltpu.make_async_copy(res.at[K : 2 * K, middle], v, done.at[1]),
        pltpu.make_async_copy(res.at[2 * K :, middle], q, done.at[2]),
    ]
    for copy in copies:
        copy.start()
    for copy in copies:
        copy.wait()


def delivered(res):
    return pl.pallas_call(
        deliver,
        out_shape=(
            jax.ShapeDtypeStruct((K, B, B), F32),
            jax.ShapeDtypeStruct((K, B, B), F32),
            jax.ShapeDtypeStruct((T * K, B, B), F32),
        ),
        in_specs=[pl.BlockSpec(memory_space=pltpu.VMEM)],
        out_specs=[pl.BlockSpec(memory_space=pltpu.HBM)] * 3,
        scratch_shapes=[pltpu.SemaphoreType.DMA((3,))],
    )(res)


def per_device(nlat, nlon, zonal_flow, meridional_flow, tracers, sea_mask, diffusivity):
    q = tracers.reshape(T * K, B, B)
    given = [
        pltpu.with_memory_space_constraint(x, pltpu.HBM)
        for x in (zonal_flow, meridional_flow, q, sea_mask, diffusivity)
    ]
    res = pltpu.with_memory_space_constraint(stepped(nlat, nlon, *given), pltpu.VMEM)
    u, v, q = delivered(res)
    return u, v, q.reshape(T, K, B, B)


def solution(mesh):
    cells = P(None, "lat", "lon")
    traced = P(None, None, "lat", "lon")
    return jax.shard_map(
        functools.partial(per_device, mesh.shape["lat"], mesh.shape["lon"]),
        mesh=mesh,
        in_specs=(cells, cells, traced, cells, cells),
        out_specs=(cells, cells, traced),
        check_vma=False,
    )
```

```python
import functools
import math

import jax
import jax.numpy as jnp
from jax import lax
from jax.experimental import pallas as pl
from jax.experimental.pallas import tpu as pltpu
from jax.sharding import PartitionSpec as P

K = 4
T = 3
NSUB = 3
B = 128
H = 8
E = B + 2 * H
R = E // 8
S = 14
DEPTH = R
WET, U, V, Q = 4, 8, 12, 16
FIELDS = (WET, U, V, Q, Q + K, Q + 2 * K)
DEPTHS = [(f, 4 if U <= f < V else 5 if V <= f < Q else 6) for f in range(WET, Q + T * K)]
ROWS = [(f, n, sum(m for _, m in DEPTHS[:i])) for i, (f, n) in enumerate(DEPTHS)]
SENT = -(-sum(n for _, n in DEPTHS) // 8) * 8
F32 = jnp.float32
MESH = pl.DeviceIdType.MESH
coriolis_peak = 0.5


def flush(pending):
    for ref, index, x in pending:
        ref[index] = x
    pending.clear()


class Batch:
    def __init__(self, parts):
        self.parts = list(parts)

    def __add__(self, other):
        return each(jnp.add, self, other)

    __radd__ = __add__

    def __sub__(self, other):
        return each(jnp.subtract, self, other)

    def __rsub__(self, other):
        return each(jnp.subtract, other, self)

    def __mul__(self, other):
        return each(jnp.multiply, self, other)

    __rmul__ = __mul__

    def __rtruediv__(self, other):
        return each(jnp.divide, other, self)

    def __neg__(self):
        return each(jnp.negative, self)

    def __gt__(self, other):
        return each(jnp.greater, self, other)


def each(function, *given):
    size = [len(x.parts) for x in given if isinstance(x, Batch)]
    if not size:
        return function(*given)
    return Batch(
        function(*(x.parts[n] if isinstance(x, Batch) else x for x in given)) for n in range(size[0])
    )


def where(mask, a, b):
    return each(jnp.where, mask, a, b)


def minmod(a, b):
    return each(jnp.maximum, each(jnp.minimum, a, b), each(jnp.minimum, each(jnp.maximum, a, b), 0.0))


def following(x):
    return each(lambda part: pltpu.roll(part, B - 1, 1), x)


def preceding(x):
    return each(lambda part: pltpu.roll(part, 1, 1), x)


def above(x):
    return pltpu.roll(x, 7, 0)


def below(x):
    return pltpu.roll(x, 1, 0)


def rolled(x, amount):
    return each(lambda part: pltpu.roll(part, amount % B, 1), x) if amount % B else x


def picked(x, index):
    return each(lambda part: jnp.take_along_axis(part, index, axis=1), x)


def merged(x, edge, k, low, high):
    lane = lax.broadcasted_iota(jnp.int32, (8, B), 1)
    source = jnp.where(lane < B // 2, lane + 32 * k + 22, lane + 32 * k + 10) % B
    return where((lane < low) | (lane >= high), picked(edge, source), x)


def flipped(x, index):
    x = jnp.take_along_axis(x, index, axis=1)
    backward = 7 - lax.broadcasted_iota(jnp.int32, (8, B), 0)
    return jnp.take_along_axis(x, backward, axis=0)


def factored(coupling):
    carried = []
    inverse = []
    for k in range(K):
        divisor = 1.0
        if k < K - 1:
            divisor = divisor + coupling[k]
        if k > 0:
            divisor = divisor + coupling[k - 1] * (1.0 - carried[k - 1])
        inverse.append(1.0 / divisor)
        if k < K - 1:
            carried.append(coupling[k] * inverse[k])
    return inverse, carried


def solve(x, coupling, inverse, carried):
    scaled = [x[0] * inverse[0]]
    for k in range(1, K):
        scaled.append((x[k] + coupling[k - 1] * scaled[k - 1]) * inverse[k])
    solved = [scaled[K - 1]]
    for k in range(K - 2, -1, -1):
        solved.insert(0, scaled[k] + carried[k] * solved[0])
    return solved


def step(
    nlat, nlon, u, v, q, m, d, res, tr, wet, dext,
    ext, mext, hn, hs, pe, pw, kn, ks, ke, kw, pn, flow, new, cx, cy, fold, cor, load, send, recv,
):
    lat = lax.axis_index("lat")
    lon = lax.axis_index("lon")
    top = lat == nlat - 1
    bottom = lat == 0
    east = lax.rem(lon + 1, nlon)
    west = lax.rem(lon + nlon - 1, nlon)
    n_lat = jnp.where(top, lat, lat + 1)
    n_mid = jnp.where(top, nlon - 1 - lon, lon)
    n_west = jnp.where(top, lax.rem(nlon - lon, nlon), west)
    n_east = jnp.where(top, lax.rem(2 * nlon - 2 - lon, nlon), east)
    s_lat = jnp.maximum(lat - 1, 0)
    own_w = n_west == lon
    own_e = n_east == lon

    def at(row, column):
        return {"lat": row, "lon": column}

    middle = pl.ds(H, B)
    beyond = pl.ds(H + B, H)
    barrier = pltpu.get_barrier_semaphore()

    def greet(row, column):
        pl.semaphore_signal(barrier, inc=1, device_id=at(row, column), device_id_type=MESH)

    lo = pl.ds(0, H)
    lo_held = pl.ds(H, H)
    hi_held = pl.ds(B, H)

    def fetch(part, held, slot):
        u_held, v_held, q_held = (ext.at[f : f + n, held] for f, n in ((U, K), (V, K), (Q, T * K)))
        return [
            pltpu.make_async_copy(u.at[:, part], u_held, load.at[slot]),
            pltpu.make_async_copy(v.at[:, part], v_held, load.at[slot + 1]),
            pltpu.make_async_copy(q.at[:, part], q_held, load.at[slot + 2]),
            pltpu.make_async_copy(m.at[:, part], mext.at[:, part], load.at[slot + 3]),
        ]

    outer_loads = fetch(lo, lo_held, 0) + fetch(pl.ds(B - H, H), hi_held, 4)
    inner_loads = fetch(pl.ds(H, B - 2 * H), pl.ds(2 * H, B - 2 * H), 8)
    inner_loads.append(pltpu.make_async_copy(d, dext.at[:, middle], load.at[12]))

    for copy in outer_loads:
        copy.start()
    greet(lat, east)
    greet(lat, west)
    greet(n_lat, n_mid)

    @pl.when(jnp.logical_not(top & own_w))
    def _():
        greet(n_lat, n_west)

    @pl.when(jnp.logical_not(top & own_e))
    def _():
        greet(n_lat, n_east)

    @pl.when(jnp.logical_not(bottom))
    def _():
        greet(s_lat, lon)
        greet(s_lat, west)
        greet(s_lat, east)

    for copy in inner_loads:
        copy.start()

    def remote(src, dst, slot, row, column):
        return pltpu.make_async_remote_copy(
            src_ref=src,
            dst_ref=dst,
            send_sem=send.at[slot],
            recv_sem=recv.at[slot],
            device_id=at(row, column),
            device_id_type=MESH,
        )


    sent, arrived = pl.ds(0, SENT), pl.ds(H, SENT)
    to_north = [remote(kn.at[sent], hs.at[arrived], 5, n_lat, n_mid)]
    over_fold = [remote(kn.at[sent], hn.at[arrived], 2, n_lat, n_mid)]
    to_south = [remote(ks.at[sent], hn.at[arrived], 2, s_lat, lon)]

    own_rows, lo_pack, hi_pack = pl.ds(H, B), pl.ds(0, 2 * H), pl.ds(B, 2 * H)
    lo_land, mid_land, hi_land = pl.ds(0, 2 * H), pl.ds(2 * H, B), pl.ds(2 * H + B, 2 * H)
    sends = [
        remote(ke.at[own_rows], pw.at[mid_land], 1, lat, east),
        remote(kw.at[own_rows], pe.at[mid_land], 0, lat, west),
    ]
    north_east = remote(ke.at[hi_pack], pw.at[lo_land], 7, n_lat, n_east)
    north_west = remote(kw.at[hi_pack], pe.at[lo_land], 6, n_lat, n_west)
    fold_west = remote(kw.at[hi_pack], pw.at[hi_land], 4, n_lat, n_west)
    fold_east = remote(ke.at[hi_pack], pe.at[hi_land], 3, n_lat, n_east)
    self_west = pltpu.make_async_copy(kw.at[hi_pack], pw.at[hi_land], load.at[13])
    self_east = pltpu.make_async_copy(ke.at[hi_pack], pe.at[hi_land], load.at[14])
    south_east = remote(ke.at[lo_pack], pw.at[hi_land], 4, s_lat, east)
    south_west = remote(kw.at[lo_pack], pe.at[hi_land], 3, s_lat, west)

    def enter():
        peers = (
            3
            + jnp.where(top & own_w, 0, 1)
            + jnp.where(top & own_e, 0, 1)
            + jnp.where(bottom, 0, 3)
        )
        pl.semaphore_wait(barrier, peers)

        @pl.when(jnp.logical_not(top))
        def _():
            north_east.start()
            north_west.start()

        @pl.when(top & own_w)
        def _():
            self_west.start()

        @pl.when(top & jnp.logical_not(own_w))
        def _():
            fold_west.start()

        @pl.when(top & own_e)
        def _():
            self_east.start()

        @pl.when(top & jnp.logical_not(own_e))
        def _():
            fold_east.start()

        @pl.when(jnp.logical_not(bottom))
        def _():
            south_east.start()
            south_west.start()

        @pl.when(top)
        def _():
            for copy in over_fold:
                copy.start()

        @pl.when(jnp.logical_not(top))
        def _():
            for copy in to_north:
                copy.start()

        @pl.when(jnp.logical_not(bottom))
        def _():
            for copy in to_south:
                copy.start()

    lane = lax.broadcasted_iota(jnp.int32, (8, B), 1)
    sub = lax.broadcasted_iota(jnp.int32, (8, B), 0)
    group = lane // 8

    reached_late = lon >= nlon // 2

    for f in range(WET, Q + T * K):
        ext[f, lo] = jnp.zeros((H, B), F32)
        ext[f, beyond] = jnp.zeros((H, B), F32)
    for landing in (hn, hs):
        landing[lo] = jnp.zeros((H, B), F32)
        landing[pl.ds(H + SENT, H)] = jnp.zeros((H, B), F32)
    for copy in outer_loads:
        copy.wait()

    place = lane % 32
    level = lane // 32
    spare_w = (place == 6) | (place == 7) | (place == 14) | (place == 15)
    spare_e = (place == 0) | (place == 1) | (place == 8) | (place == 9)
    spare_of = jnp.where(
        spare_w,
        jnp.where(place < 8, place - 6, place - 12),
        jnp.where(place < 8, B - 4 + place, B - 10 + place),
    )
    spare_of = jnp.minimum(spare_of, B - 1)

    held_blocks = [pl.ds(i * 8 + H, 8) for i in range(B // 8)]
    inner_blocks = held_blocks[1:-1]
    outer_blocks = [lo_held, hi_held]

    def read(ref, *index, parts=held_blocks):
        return Batch(ref[(*index, part)] for part in parts)

    pending = []

    def write(ref, index, x, parts=held_blocks):
        for part, y in zip(parts, x.parts, strict=True):
            pending.append((ref, (*index, part), y))

    def convert(parts):
        for k in range(K):
            for part in parts:
                pending.append((ext, (WET + k, part), mext[k, pl.ds(part.start - H, 8)].astype(F32)))
        flush(pending)

    def pack(parts):
        packed_w = packed_e = Batch([jnp.zeros((8, B), F32)] * len(parts))
        for k in range(K):
            for f, field in enumerate((Q, Q + K, Q + 2 * K, WET)):
                j = 4 * k + f
                x = rolled(read(ext, field + k, parts=parts), 8 * j)
                packed_w = where(group == j, x, packed_w)
                packed_e = where(group == (j - 1) % 16, x, packed_e)
            x = picked(read(ext, V + k, parts=parts), spare_of)
            packed_w = where(spare_w & (level == k), x, packed_w)
            packed_e = where(spare_e & (level == k), x, packed_e)
        write(kw, (), packed_w, parts)
        write(ke, (), packed_e, parts)

    def pack_flow(parts, into):
        packed_w = packed_e = Batch([jnp.zeros((8, B), F32)] * len(parts))
        for k in range(K):
            for f, field in enumerate((U, V)):
                j = 4 * k + f
                x = rolled(read(ext, field + k, parts=parts), 8 * j)
                packed_w = where(group == j, x, packed_w)
                packed_e = where(group == (j - 1) % 16, x, packed_e)
        write(kw, (), packed_w, into)
        write(ke, (), packed_e, into)

    convert(outer_blocks)
    pack(outer_blocks)
    pack_flow(outer_blocks, [lo, beyond])
    flush(pending)
    for f, n, at in ROWS:
        kn[pl.ds(at, 8)] = ext[f, pl.ds(H + B - n, 8)]
        ks[pl.ds(at, 8)] = ext[f, lo_held]

    @pl.when(reached_late)
    def _():
        enter()

    for copy in inner_loads:
        copy.wait()
    convert(inner_blocks)
    pack(inner_blocks)
    flush(pending)

    @pl.when(reached_late)
    def _():
        for copy in sends:
            copy.start()

    far_hi = (place >= 10) & (place < 16)
    far_lo = (place >= 16) & (place < 22)
    source_of = (place + jnp.where(place < 16, 118, B - 22)) % B

    def edges(field, parts):
        edge = picked(Batch(ext[field, part] for part in parts), source_of)
        for k in range(1, K):
            x = picked(Batch(ext[field + k, part] for part in parts), source_of)
            edge = where(level == k, x, edge)
        return edge

    for n, field in enumerate(FIELDS):
        write(pn, (n,), edges(field, held_blocks))
        flush(pending)

    def keep(n, i, r, x):
        ref, index = (wet, (i, r)) if n == 0 else (flow, (n - 1, i, r)) if n < 3 else (tr, (n - 3, i, r))
        pending.append((ref, index, x))

    def levels(n, r):
        for k in range(K):
            keep(n, k, r, ext[FIELDS[n] + k, pl.ds(r, 8, stride=R)])

    for r in range(R):
        for n in range(len(FIELDS)):
            levels(n, r)
        flush(pending)

    @pl.when(jnp.logical_not(reached_late))
    def _():
        enter()
        for copy in sends:
            copy.start()

    def coriolis(offset):
        row = lat * B + R * sub + lane - H
        ny = nlat * B
        return coriolis_peak * jnp.sin(math.pi * ((row.astype(F32) + offset) / ny - 0.5))

    for f, offset in enumerate((0.5, 1.0)):
        turning = coriolis(offset)
        for r in range(R):
            cor[f, r] = jnp.broadcast_to(turning[:, r : r + 1], (8, B))

    def prepare(cells, count, bend, beyond_fold, momentum, size=9):
        def get(f, i, r):
            if r == -1:
                return below(flow[f, i, count - 1])
            if r == count:
                return above(flow[f, i, 0])
            return flow[f, i, r]

        for start in range(0, len(cells), size):
            chunk = cells[start : start + size]

            def put(ref, index, x):
                for (i, r), y in zip(chunk, x.parts, strict=True):
                    held_back.append((ref, (index, i, r), y))

            def bent(a, b):
                return Batch(
                    jnp.where(beyond_fold, x, y) if r > bend else y
                    for (_, r), x, y in zip(chunk, a.parts, b.parts, strict=True)
                )

            held_back = []
            u0, v0 = (Batch(get(f, i, r) for i, r in chunk) for f in range(2))
            un, vn = (Batch(get(f, i, r + 1) for i, r in chunk) for f in range(2))
            w0 = Batch(wet[i, r] for i, r in chunk)
            wn = Batch(wet[i, r + 1] if r < count - 1 else above(wet[i, 0]) for i, r in chunk)
            gu = w0 * following(w0)
            gv = w0 * wn
            ue = following(u0)
            uw = preceding(u0)
            gw = preceding(gu)
            ua = bent(ue, u0)
            wa = bent(u0, uw)
            va = bent(vn, v0)
            put(cx, 0, gu)
            put(cx, 1, each(jnp.maximum, ua, 0.0) * gu)
            put(cx, 2, 0.5 - 0.5 * ua)
            put(cx, 3, gw)
            put(cx, 4, each(jnp.minimum, wa, 0.0) * gw)
            put(cx, 5, -0.5 - 0.5 * wa)
            put(cy, 0, gv)
            put(cy, 1, va * gv)
            put(cy, 2, where(va > 0.0, 0.5, -0.5) - 0.5 * va)
            for n, (i, r) in enumerate(chunk):
                if r == bend:
                    vf = jnp.where(beyond_fold, vn.parts[n], v0.parts[n])
                    held_back.append((fold, (0, i), vf * gv.parts[n]))
                    held_back.append((fold, (1, i), jnp.where(vf > 0.0, 0.5, -0.5) - 0.5 * vf))
            if momentum:
                us, vs = (Batch(get(f, i, r - 1) for i, r in chunk) for f in range(2))
                turn_u, turn_v = (Batch(cor[f, r] for _, r in chunk) for f in range(2))
                a = v0 + vs
                vbar = 0.25 * (a + following(a))
                a = u0 + un
                ubar = 0.25 * (a + preceding(a))
                du = vbar * (turn_u - 0.5 * (un - us)) - 0.5 * u0 * (ue - uw)
                dv = -ubar * (turn_v + 0.5 * (following(v0) - preceding(v0))) - 0.5 * v0 * (vn - vs)
                put(new, 0, u0 + gu * du)
                put(new, 1, v0 + gv * dv)
            flush(held_back)

    last = top & (sub == 7)
    last_strip = top & (sub >= 4)
    bend = R - H - 1

    def prepare_level(rows, i, carry):
        prepare([(i, r) for r in rows], R, bend, last, True)
        return carry

    lax.fori_loop(0, K, functools.partial(prepare_level, range(R)), 0)

    def face(w, c, here, there, slope_here, slope_there):
        way = w > 0.0
        return w * (jnp.where(way, here, there) + c * jnp.where(way, slope_here, slope_there))

    def advect(i, count, bend):
        first, held_back = [None] * T, []
        turned, last_jump, last_slope = [], [], []
        now, ahead, jump, slope, south = [], [], [], [], []
        for t in range(T):
            x0, x1 = tr[t, i, 0], tr[t, i, 1]
            xr = above(x0)
            jr = (xr - tr[t, i, count - 1]) * cy[0, i, count - 1]
            j0 = (x1 - x0) * cy[0, i, 0]
            s0 = minmod(j0, below(jr))
            turned.append(xr)
            last_jump.append(jr)
            last_slope.append(above(s0))
            now.append(x0)
            ahead.append(x1)
            jump.append(j0)
            slope.append(s0)
            south.append(None)
        state = {}

        def stage_a(t, r):
            x = tr[t, i, r]
            state[t, r] = (following(x), preceding(x))

        def stage_b(t, r):
            e, p = state[t, r]
            x = tr[t, i, r]
            s = minmod((e - x) * cx[0, i, r], (x - p) * cx[3, i, r])
            a = cx[1, i, r] * (x + cx[2, i, r] * s)
            b = cx[4, i, r] * (x + cx[5, i, r] * s)
            state[t, r] = (b - a, preceding(a), following(b))

        def stage_e(t, r):
            own, a, b = state.pop((t, r))
            x, xn = now[t], ahead[t]
            if r + 1 < count - 1:
                xnn = tr[t, i, r + 2]
                jn = (xnn - xn) * cy[0, i, r + 1]
                sn = minmod(jn, jump[t])
            elif r + 1 == count - 1:
                xnn = turned[t]
                jn = last_jump[t]
                sn = minmod(jn, jump[t])
            else:
                xnn = jn = None
                sn = last_slope[t]
            north = face(cy[1, i, r], cy[2, i, r], x, xn, slope[t], sn)
            y = x - north if r == 0 else x - (north - south[t])
            if r == bend:
                north = face(fold[0, i], fold[1, i], x, xn, slope[t], sn)
            south[t] = north
            now[t], ahead[t], jump[t], slope[t] = xn, xnn, jn, sn
            y = y + (own + (a - b))
            if r == 0:
                first[t] = y
            else:
                held_back.append((tr, (t, i, r), y))

        stages = [stage_a, stage_b, stage_e]
        for tick in range(count + 2 * DEPTH):
            for n in (2, 1, 0):
                r = tick - n * DEPTH
                if 0 <= r < count:
                    for t in range(T):
                        stages[n](t, r)
            if tick % 3 == 2:
                flush(held_back)
        flush(held_back)
        for t in range(T):
            tr[t, i, 0] = first[t] + below(south[t])

    def advect_level(i, carry):
        advect(lax.rem(i, K + 1), R, bend)
        return carry

    def advect_inner(i, carry):
        advect(lax.rem(i, K), R, bend)
        return carry

    lax.fori_loop(0, 2 * K, advect_inner, 0)

    for copy in sends:
        copy.wait_send()

    @pl.when(top)
    def _():
        for copy in over_fold:
            copy.wait_send()

    @pl.when(jnp.logical_not(top))
    def _():
        for copy in to_north:
            copy.wait_send()
        north_east.wait_send()
        north_west.wait_send()

    @pl.when(top & own_w)
    def _():
        self_west.wait()

    @pl.when(top & jnp.logical_not(own_w))
    def _():
        fold_west.wait_send()

    @pl.when(top & own_e)
    def _():
        self_east.wait()

    @pl.when(top & jnp.logical_not(own_e))
    def _():
        fold_east.wait_send()

    @pl.when(jnp.logical_not(bottom))
    def _():
        for copy in to_south:
            copy.wait_send()
        south_east.wait_send()
        south_west.wait_send()

    for copy in sends:
        copy.wait_recv()
    for copy in to_south:
        copy.wait_recv()

    @pl.when(jnp.logical_not(top & own_w))
    def _():
        south_east.wait_recv()

    @pl.when(jnp.logical_not(top & own_e))
    def _():
        south_west.wait_recv()

    @pl.when(jnp.logical_not(bottom))
    def _():
        for copy in to_north:
            copy.wait_recv()
        north_east.wait_recv()
        north_west.wait_recv()


    for f, n, at in ROWS:
        pending.append((ext, (f, lo), hs[pl.ds(at + n, 8)]))
        pending.append((ext, (f, beyond), hn[pl.ds(at + H, 8)]))
    flush(pending)

    @pl.when(bottom)
    def _():
        for f in range(WET, Q + T * K):
            ext[f, lo] = jnp.zeros((H, B), F32)
        pe[lo_land] = jnp.zeros((2 * H, B), F32)
        pw[lo_land] = jnp.zeros((2 * H, B), F32)

    @pl.when(top)
    def _():
        whole = B - 1 - lane
        turned = [flipped(hn[pl.ds(at + n, 8)], whole) for _, n, at in ROWS]
        for f, x in enumerate(turned, WET):
            ext[f, beyond] = -x if U <= f < Q else x
        within = 7 - lane % 8
        from_east = (lane // 8 + 15) % 16 * 8 + within
        from_west = (lane // 8 + 1) % 16 * 8 + within
        first, second = pl.ds(2 * H + B, H), pl.ds(3 * H + B, H)
        for landed, source in ((pe, from_east), (pw, from_west)):
            x, y = flipped(landed[first], source), flipped(landed[second], source)
            landed[first] = -y
            landed[second] = x

    def spread(n, parts, pack_e, pack_w, slot, own):
        x = where(far_hi, rolled(pack_e, 10 - 8 * slot), own)
        x = where(far_lo, rolled(pack_w, 22 - 8 * slot), x)
        for part, y in zip(parts, x.parts, strict=True):
            pending.append((pn, (n, part), y))

    corners = ((lo, beyond), (lo, pl.ds(3 * H + B, H)), (pl.ds(H, H), pl.ds(2 * H + B, H)))
    order = ((0, 3), (3, 0), (4, 1), (5, 2), (1, 0), (2, 1))
    landings = [corners[2] if n in (1, 2) else corners[1] for n, _ in order]
    far = [
        [rolled(Batch(pack[part] for part in landed), offset - 8 * slot) for landed, (_, slot) in zip(landings, order)]
        for pack, offset in ((pe, 10), (pw, 22))
    ]
    picks = [
        [picked(Batch(ext[FIELDS[n] + k, part] for part in corners[0]), source_of) for k in range(K)] for n, _ in order
    ]
    for (n, _), x, far_e, far_w in zip(order, picks, *far):
        edge = x[0]
        for k in range(1, K):
            edge = where(level == k, x[k], edge)
        edge = where(far_lo, far_w, where(far_hi, far_e, edge))
        for part, y in zip(corners[0], edge.parts, strict=True):
            pending.append((pn, (n, part), y))
    landed = [pl.ds(i * 8 + 2 * H, 8) for i in range(B // 8)]
    pack_e, pack_w = (Batch(pack[part] for part in landed) for pack in (pe, pw))
    for n, slot in ((0, 3), (3, 0), (4, 1), (5, 2)):
        spread(n, held_blocks, pack_e, pack_w, slot, read(pn, n))
    from_spare_e = jnp.where(place < 12, lane - 4, lane + 2)
    from_spare_w = jnp.where(place < 20, lane - 18, lane - 12)
    from_spare = jnp.where(place < 16, from_spare_e, from_spare_w) % B
    x = where(far_hi, picked(pack_e, from_spare), read(pn, 2))
    far_v = where(far_lo, picked(pack_w, from_spare), x)
    write(pn, (2,), far_v)
    flush(pending)
    run_hi = (place >= 9) & (place < 14)
    run_lo = (place >= 17) & (place < 23)
    own = read(pn, 1)
    dv = far_v - Batch(pn[2, pl.ds(i * 8 + H - 1, 8)] for i in range(B // 8))
    x = where(run_hi, where(place == 9, own, -dv), 0.0)
    y = where(run_lo, where(place == 22, own, rolled(dv, -1)), 0.0)
    x2, y2 = x + rolled(x, 1), y + rolled(y, -1)
    x, y = x2 + rolled(x2, 2) + rolled(x, 4), y2 + rolled(y2, -2) + rolled(y2, -4)
    write(pn, (1,), where(far_hi, x, where(far_lo, y, own)))
    flush(pending)
    for r in range(R):
        for n in range(len(FIELDS)):
            keep(n, K, r, pn[n, pl.ds(r, 8, stride=R)])
        flush(pending)

    flat = ext.reshape(32 * E, B)
    for r in range(S):
        for n, field in enumerate(FIELDS):
            south_rows = flat[pl.ds(field * E + H - 6 + r, 8, stride=E), :]
            north_rows = flat[pl.ds((field - K) * E + H + 120 + r, 8, stride=E), :]
            keep(n, K + 1, r, jnp.where(sub < 4, south_rows, north_rows))
        flush(pending)

    for r in (6, 7, 10, 11):
        for n in range(3):
            levels(n, r)
        flush(pending)
    prepare([(K, r) for r in range(R)], R, bend, last, True, R)
    prepare([(K + 1, r) for r in range(S)], S, 7, last_strip, False, S)
    prepare([(k, r) for k in range(K) for r in range(6, 11)], R, bend, last, True, 20)

    def advect_edges(i, carry):
        advect(K, R, bend)
        advect(K + 1, S, 7)
        return carry

    lax.fori_loop(0, 2, advect_edges, 0)

    ends = (sub == 0) | (sub == 7)
    for t in range(T):
        strip = [
            jnp.take_along_axis(tr[t, K + 1, r - 2], jnp.where(sub == 0, k, 4 + k), axis=0)
            for k in range(K)
            for r in range(6, 12)
        ]
        edge = Batch(tr[t, K, r] for r in range(R))
        x = [
            [jnp.where(ends, strip[6 * k + r - 6], tr[t, k, r]) if 6 <= r < 12 else tr[t, k, r] for r in range(R)]
            for k in range(K)
        ]
        x = [merged(Batch(x[k]), edge, k, 4, B - 4) for k in range(K)]
        for k in range(K):
            for r in range(R):
                pending.append((tr, (t, k, r), x[k].parts[r]))
        flush(pending)

    lax.fori_loop(0, K + 1, advect_level, 0)

    for start in range(0, R, 6):
        strided = [pl.ds(r, 8, stride=R) for r in range(start, start + 6)]

        def rows_of(ref, *index):
            return Batch(ref[(*index, r)] for r in range(start, start + 6))

        def both(ref, first, k, low, high):
            return merged(rows_of(ref, *first, k), rows_of(ref, *first, K), k, low, high)

        def leave(first, solved):
            for k in range(K):
                for part, x in zip(strided, solved[k].parts, strict=True):
                    pending.append((res, (first + k, part), x))

        mix = [Batch(dext[k, part] for part in strided) for k in range(K - 1)]
        gu = [both(cx, (0,), k, 0, B - 1) for k in range(K)]
        un = [both(new, (0,), k, 1, B - 1) for k in range(K)]
        coupling = [mix[k] * (gu[k] * gu[k + 1]) for k in range(K - 1)]
        un = solve(un, coupling, *factored(coupling))
        leave(0, un)
        gv = [rows_of(cy, 0, k) for k in range(K)]
        vn = [both(new, (1,), k, 1, B - 1) for k in range(K)]
        coupling = [mix[k] * (gv[k] * gv[k + 1]) for k in range(K - 1)]
        vn = solve(vn, coupling, *factored(coupling))
        leave(K, vn)
        flush(pending)


def stepped(nlat, nlon, u, v, q, m, d):
    hbm = pl.BlockSpec(memory_space=pltpu.HBM)
    return pl.pallas_call(
        functools.partial(step, nlat, nlon),
        out_shape=[
            jax.ShapeDtypeStruct((2 * K, E, B), F32),
            jax.ShapeDtypeStruct((T, K + 2, R, 8, B), F32),
            jax.ShapeDtypeStruct((K + 2, R, 8, B), F32),
            jax.ShapeDtypeStruct((K - 1, E, B), F32),
        ],
        in_specs=[hbm] * 5,
        out_specs=[pl.BlockSpec(memory_space=pltpu.VMEM)] * 4,
        scratch_shapes=[
            pltpu.VMEM((32, E, B), F32),
            pltpu.VMEM((K, B, B), jnp.int32),
            pltpu.VMEM((SENT + 2 * H, B), F32),
            pltpu.VMEM((SENT + 2 * H, B), F32),
            pltpu.VMEM((B + 4 * H, B), F32),
            pltpu.VMEM((B + 4 * H, B), F32),
            pltpu.VMEM((SENT + H, B), F32),
            pltpu.VMEM((SENT + H, B), F32),
            pltpu.VMEM((E, B), F32),
            pltpu.VMEM((E, B), F32),
            pltpu.VMEM((len(FIELDS), E, B), F32),
            pltpu.VMEM((2, K + 2, R, 8, B), F32),
            pltpu.VMEM((2, K + 1, R, 8, B), F32),
            pltpu.VMEM((6, K + 2, R, 8, B), F32),
            pltpu.VMEM((3, K + 2, R, 8, B), F32),
            pltpu.VMEM((2, K + 2, 8, B), F32),
            pltpu.VMEM((2, R, 8, B), F32),
            pltpu.SemaphoreType.DMA((15,)),
            pltpu.SemaphoreType.DMA((8,)),
            pltpu.SemaphoreType.DMA((8,)),
        ],
        compiler_params=pltpu.CompilerParams(
            collective_id=0, has_side_effects=True, vmem_limit_bytes=40 * 2**20
        ),
    )(u, v, q, m, d)


def deliver(res, tr, wet, dext, u, v, q, out, done):
    middle = pl.ds(H, B)
    copies = [
        pltpu.make_async_copy(res.at[0:K, middle], u, done.at[0]),
        pltpu.make_async_copy(res.at[K : 2 * K, middle], v, done.at[1]),
    ]
    for copy in copies:
        copy.start()
    factors = []
    for start in range(0, R, 6):
        rows = range(start, start + 6)
        w = [Batch(wet[k, r] for r in rows) for k in range(K)]
        mix = [Batch(dext[k, pl.ds(r, 8, stride=R)] for r in rows) for k in range(K - 1)]
        coupling = [mix[k] * (w[k] * w[k + 1]) for k in range(K - 1)]
        factors.append((rows, coupling, *factored(coupling)))
    for t in range(T):
        for rows, *factor in factors:
            edge = Batch(tr[t, K, r] for r in rows)
            x = [merged(Batch(tr[t, k, r] for r in rows), edge, k, 2, B - 2) for k in range(K)]
            for k, solved in enumerate(solve(x, *factor)):
                for r, y in zip(rows, solved.parts, strict=True):
                    out[t * K + k, pl.ds(r, 8, stride=R)] = y
        part = pl.ds(t * K, K)
        copies.append(pltpu.make_async_copy(out.at[part, middle], q.at[part], done.at[2 + t]))
        copies[-1].start()
    for copy in copies:
        copy.wait()


def delivered(given):
    return pl.pallas_call(
        deliver,
        out_shape=(
            jax.ShapeDtypeStruct((K, B, B), F32),
            jax.ShapeDtypeStruct((K, B, B), F32),
            jax.ShapeDtypeStruct((T * K, B, B), F32),
        ),
        in_specs=[pl.BlockSpec(memory_space=pltpu.VMEM)] * 4,
        out_specs=[pl.BlockSpec(memory_space=pltpu.HBM)] * 3,
        scratch_shapes=[pltpu.VMEM((T * K, E, B), F32), pltpu.SemaphoreType.DMA((2 + T,))],
    )(*given)


def per_device(nlat, nlon, zonal_flow, meridional_flow, tracers, sea_mask, diffusivity):
    q = tracers.reshape(T * K, B, B)
    given = [
        pltpu.with_memory_space_constraint(x, pltpu.HBM)
        for x in (zonal_flow, meridional_flow, q, sea_mask, diffusivity)
    ]
    kept = [pltpu.with_memory_space_constraint(x, pltpu.VMEM) for x in stepped(nlat, nlon, *given)]
    u, v, q = delivered(kept)
    return u, v, q.reshape(T, K, B, B)


def solution(mesh):
    cells = P(None, "lat", "lon")
    traced = P(None, None, "lat", "lon")
    return jax.shard_map(
        functools.partial(per_device, mesh.shape["lat"], mesh.shape["lon"]),
        mesh=mesh,
        in_specs=(cells, cells, traced, cells, cells),
        out_specs=(cells, cells, traced),
        check_vma=False,
    )
```

```python
import functools
import math

import jax
import jax.numpy as jnp
from jax import lax
from jax.experimental import pallas as pl
from jax.experimental.pallas import tpu as pltpu
from jax.sharding import PartitionSpec as P

K = 4
T = 3
NSUB = 3
B = 128
H = 8
E = B + 2 * H
R = E // 8
S = 14
DEPTH = R
WET, U, V, Q = 4, 8, 12, 16
FIELDS = (WET, U, V, Q, Q + K, Q + 2 * K)
DEPTHS = [(f, 4 if U <= f < V else 5 if V <= f < Q else 6) for f in range(WET, Q + T * K)]
ROWS = [(f, n, sum(m for _, m in DEPTHS[:i])) for i, (f, n) in enumerate(DEPTHS)]
SENT = -(-sum(n for _, n in DEPTHS) // 8) * 8
F32 = jnp.float32
MESH = pl.DeviceIdType.MESH
coriolis_peak = 0.5


def flush(pending):
    for ref, index, x in pending:
        ref[index] = x
    pending.clear()


class Batch:
    def __init__(self, parts):
        self.parts = list(parts)

    def __add__(self, other):
        return each(jnp.add, self, other)

    __radd__ = __add__

    def __sub__(self, other):
        return each(jnp.subtract, self, other)

    def __rsub__(self, other):
        return each(jnp.subtract, other, self)

    def __mul__(self, other):
        return each(jnp.multiply, self, other)

    __rmul__ = __mul__

    def __rtruediv__(self, other):
        return each(jnp.divide, other, self)

    def __neg__(self):
        return each(jnp.negative, self)

    def __gt__(self, other):
        return each(jnp.greater, self, other)


def each(function, *given):
    size = [len(x.parts) for x in given if isinstance(x, Batch)]
    if not size:
        return function(*given)
    return Batch(
        function(*(x.parts[n] if isinstance(x, Batch) else x for x in given)) for n in range(size[0])
    )


def where(mask, a, b):
    return each(jnp.where, mask, a, b)


def minmod(a, b):
    return each(jnp.maximum, each(jnp.minimum, a, b), each(jnp.minimum, each(jnp.maximum, a, b), 0.0))


def following(x):
    return each(lambda part: pltpu.roll(part, B - 1, 1), x)


def preceding(x):
    return each(lambda part: pltpu.roll(part, 1, 1), x)


def above(x):
    return pltpu.roll(x, 7, 0)


def below(x):
    return pltpu.roll(x, 1, 0)


def rolled(x, amount):
    return each(lambda part: pltpu.roll(part, amount % B, 1), x) if amount % B else x


def picked(x, index):
    return each(lambda part: jnp.take_along_axis(part, index, axis=1), x)


def merged(x, edge, k, low, high):
    lane = lax.broadcasted_iota(jnp.int32, (8, B), 1)
    source = jnp.where(lane < B // 2, lane + 32 * k + 22, lane + 32 * k + 10) % B
    return where((lane < low) | (lane >= high), picked(edge, source), x)


def flipped(x, index):
    x = jnp.take_along_axis(x, index, axis=1)
    backward = 7 - lax.broadcasted_iota(jnp.int32, (8, B), 0)
    return jnp.take_along_axis(x, backward, axis=0)


def factored(coupling):
    carried = []
    inverse = []
    for k in range(K):
        divisor = 1.0
        if k < K - 1:
            divisor = divisor + coupling[k]
        if k > 0:
            divisor = divisor + coupling[k - 1] * (1.0 - carried[k - 1])
        inverse.append(1.0 / divisor)
        if k < K - 1:
            carried.append(coupling[k] * inverse[k])
    return inverse, carried


def solve(x, coupling, inverse, carried):
    scaled = [x[0] * inverse[0]]
    for k in range(1, K):
        scaled.append((x[k] + coupling[k - 1] * scaled[k - 1]) * inverse[k])
    solved = [scaled[K - 1]]
    for k in range(K - 2, -1, -1):
        solved.insert(0, scaled[k] + carried[k] * solved[0])
    return solved


def step(
    nlat, nlon, u, v, q, m, d, res, tr, wet, dext,
    ext, mext, hn, hs, pe, pw, kn, ks, ke, kw, pn, flow, new, cx, cy, fold, cor, load, send, recv,
):
    lat = lax.axis_index("lat")
    lon = lax.axis_index("lon")
    top = lat == nlat - 1
    bottom = lat == 0
    east = lax.rem(lon + 1, nlon)
    west = lax.rem(lon + nlon - 1, nlon)
    n_lat = jnp.where(top, lat, lat + 1)
    n_mid = jnp.where(top, nlon - 1 - lon, lon)
    n_west = jnp.where(top, lax.rem(nlon - lon, nlon), west)
    n_east = jnp.where(top, lax.rem(2 * nlon - 2 - lon, nlon), east)
    s_lat = jnp.maximum(lat - 1, 0)
    own_w = n_west == lon
    own_e = n_east == lon

    def at(row, column):
        return {"lat": row, "lon": column}

    middle = pl.ds(H, B)
    beyond = pl.ds(H + B, H)
    barrier = pltpu.get_barrier_semaphore()

    def greet(row, column):
        pl.semaphore_signal(barrier, inc=1, device_id=at(row, column), device_id_type=MESH)

    lo = pl.ds(0, H)
    lo_held = pl.ds(H, H)
    hi_held = pl.ds(B, H)

    def fetch(part, held, slot):
        u_held, v_held, q_held = (ext.at[f : f + n, held] for f, n in ((U, K), (V, K), (Q, T * K)))
        return [
            pltpu.make_async_copy(u.at[:, part], u_held, load.at[slot]),
            pltpu.make_async_copy(v.at[:, part], v_held, load.at[slot + 1]),
            pltpu.make_async_copy(q.at[:, part], q_held, load.at[slot + 2]),
            pltpu.make_async_copy(m.at[:, part], mext.at[:, part], load.at[slot + 3]),
        ]

    outer_loads = fetch(lo, lo_held, 0) + fetch(pl.ds(B - H, H), hi_held, 4)
    inner_loads = fetch(pl.ds(H, B - 2 * H), pl.ds(2 * H, B - 2 * H), 8)
    inner_loads.append(pltpu.make_async_copy(d, dext.at[:, middle], load.at[12]))

    for copy in outer_loads:
        copy.start()
    greet(lat, east)
    greet(lat, west)
    greet(n_lat, n_mid)

    @pl.when(jnp.logical_not(top & own_w))
    def _():
        greet(n_lat, n_west)

    @pl.when(jnp.logical_not(top & own_e))
    def _():
        greet(n_lat, n_east)

    @pl.when(jnp.logical_not(bottom))
    def _():
        greet(s_lat, lon)
        greet(s_lat, west)
        greet(s_lat, east)

    for copy in inner_loads:
        copy.start()

    def remote(src, dst, slot, row, column):
        return pltpu.make_async_remote_copy(
            src_ref=src,
            dst_ref=dst,
            send_sem=send.at[slot],
            recv_sem=recv.at[slot],
            device_id=at(row, column),
            device_id_type=MESH,
        )


    sent, arrived = pl.ds(0, SENT), pl.ds(H, SENT)
    to_north = [remote(kn.at[sent], hs.at[arrived], 5, n_lat, n_mid)]
    over_fold = [remote(kn.at[sent], hn.at[arrived], 2, n_lat, n_mid)]
    to_south = [remote(ks.at[sent], hn.at[arrived], 2, s_lat, lon)]

    own_rows, lo_pack, hi_pack = pl.ds(H, B), pl.ds(0, 2 * H), pl.ds(B, 2 * H)
    lo_land, mid_land, hi_land = pl.ds(0, 2 * H), pl.ds(2 * H, B), pl.ds(2 * H + B, 2 * H)
    sends = [
        remote(ke.at[own_rows], pw.at[mid_land], 1, lat, east),
        remote(kw.at[own_rows], pe.at[mid_land], 0, lat, west),
    ]
    north_east = remote(ke.at[hi_pack], pw.at[lo_land], 7, n_lat, n_east)
    north_west = remote(kw.at[hi_pack], pe.at[lo_land], 6, n_lat, n_west)
    fold_west = remote(kw.at[hi_pack], pw.at[hi_land], 4, n_lat, n_west)
    fold_east = remote(ke.at[hi_pack], pe.at[hi_land], 3, n_lat, n_east)
    self_west = pltpu.make_async_copy(kw.at[hi_pack], pw.at[hi_land], load.at[13])
    self_east = pltpu.make_async_copy(ke.at[hi_pack], pe.at[hi_land], load.at[14])
    south_east = remote(ke.at[lo_pack], pw.at[hi_land], 4, s_lat, east)
    south_west = remote(kw.at[lo_pack], pe.at[hi_land], 3, s_lat, west)

    def enter():
        peers = (
            3
            + jnp.where(top & own_w, 0, 1)
            + jnp.where(top & own_e, 0, 1)
            + jnp.where(bottom, 0, 3)
        )
        pl.semaphore_wait(barrier, peers)

        @pl.when(jnp.logical_not(top))
        def _():
            north_east.start()
            north_west.start()

        @pl.when(top & own_w)
        def _():
            self_west.start()

        @pl.when(top & jnp.logical_not(own_w))
        def _():
            fold_west.start()

        @pl.when(top & own_e)
        def _():
            self_east.start()

        @pl.when(top & jnp.logical_not(own_e))
        def _():
            fold_east.start()

        @pl.when(jnp.logical_not(bottom))
        def _():
            south_east.start()
            south_west.start()

        @pl.when(top)
        def _():
            for copy in over_fold:
                copy.start()

        @pl.when(jnp.logical_not(top))
        def _():
            for copy in to_north:
                copy.start()

        @pl.when(jnp.logical_not(bottom))
        def _():
            for copy in to_south:
                copy.start()

    lane = lax.broadcasted_iota(jnp.int32, (8, B), 1)
    sub = lax.broadcasted_iota(jnp.int32, (8, B), 0)
    group = lane // 8

    reached_late = lon >= nlon // 2

    for f in range(WET, Q + T * K):
        ext[f, lo] = jnp.zeros((H, B), F32)
        ext[f, beyond] = jnp.zeros((H, B), F32)
    for landing in (hn, hs):
        landing[lo] = jnp.zeros((H, B), F32)
        landing[pl.ds(H + SENT, H)] = jnp.zeros((H, B), F32)
    for copy in outer_loads:
        copy.wait()

    place = lane % 32
    level = lane // 32
    spare_w = (place == 6) | (place == 7) | (place == 14) | (place == 15)
    spare_e = (place == 0) | (place == 1) | (place == 8) | (place == 9)
    spare_of = jnp.where(
        spare_w,
        jnp.where(place < 8, place - 6, place - 12),
        jnp.where(place < 8, B - 4 + place, B - 10 + place),
    )
    spare_of = jnp.minimum(spare_of, B - 1)

    held_blocks = [pl.ds(i * 8 + H, 8) for i in range(B // 8)]
    inner_blocks = held_blocks[1:-1]
    outer_blocks = [lo_held, hi_held]

    def read(ref, *index, parts=held_blocks):
        return Batch(ref[(*index, part)] for part in parts)

    pending = []

    def write(ref, index, x, parts=held_blocks):
        for part, y in zip(parts, x.parts, strict=True):
            pending.append((ref, (*index, part), y))

    def convert(parts):
        for k in range(K):
            for part in parts:
                pending.append((ext, (WET + k, part), mext[k, pl.ds(part.start - H, 8)].astype(F32)))
        flush(pending)

    def pack(parts):
        packed_w = packed_e = Batch([jnp.zeros((8, B), F32)] * len(parts))
        for k in range(K):
            for f, field in enumerate((Q, Q + K, Q + 2 * K, WET)):
                j = 4 * k + f
                x = rolled(read(ext, field + k, parts=parts), 8 * j)
                packed_w = where(group == j, x, packed_w)
                packed_e = where(group == (j - 1) % 16, x, packed_e)
            x = picked(read(ext, V + k, parts=parts), spare_of)
            packed_w = where(spare_w & (level == k), x, packed_w)
            packed_e = where(spare_e & (level == k), x, packed_e)
        write(kw, (), packed_w, parts)
        write(ke, (), packed_e, parts)

    def pack_flow(parts, into):
        packed_w = packed_e = Batch([jnp.zeros((8, B), F32)] * len(parts))
        for k in range(K):
            for f, field in enumerate((U, V)):
                j = 4 * k + f
                x = rolled(read(ext, field + k, parts=parts), 8 * j)
                packed_w = where(group == j, x, packed_w)
                packed_e = where(group == (j - 1) % 16, x, packed_e)
        write(kw, (), packed_w, into)
        write(ke, (), packed_e, into)

    convert(outer_blocks)
    pack(outer_blocks)
    pack_flow(outer_blocks, [lo, beyond])
    flush(pending)
    for f, n, at in ROWS:
        kn[pl.ds(at, 8)] = ext[f, pl.ds(H + B - n, 8)]
        ks[pl.ds(at, 8)] = ext[f, lo_held]

    @pl.when(reached_late)
    def _():
        enter()

    for copy in inner_loads:
        copy.wait()
    convert(inner_blocks)
    pack(inner_blocks)
    flush(pending)

    @pl.when(reached_late)
    def _():
        for copy in sends:
            copy.start()

    far_hi = (place >= 10) & (place < 16)
    far_lo = (place >= 16) & (place < 22)
    source_of = (place + jnp.where(place < 16, 118, B - 22)) % B

    def edges(field, parts):
        edge = picked(Batch(ext[field, part] for part in parts), source_of)
        for k in range(1, K):
            x = picked(Batch(ext[field + k, part] for part in parts), source_of)
            edge = where(level == k, x, edge)
        return edge

    for n, field in enumerate(FIELDS):
        write(pn, (n,), edges(field, held_blocks))
        flush(pending)

    def keep(n, i, r, x):
        ref, index = (wet, (i, r)) if n == 0 else (flow, (n - 1, i, r)) if n < 3 else (tr, (n - 3, i, r))
        pending.append((ref, index, x))

    def levels(n, r):
        for k in range(K):
            keep(n, k, r, ext[FIELDS[n] + k, pl.ds(r, 8, stride=R)])

    for r in range(R):
        for n in range(len(FIELDS)):
            levels(n, r)
        flush(pending)

    @pl.when(jnp.logical_not(reached_late))
    def _():
        enter()
        for copy in sends:
            copy.start()

    def coriolis(offset):
        row = lat * B + R * sub + lane - H
        ny = nlat * B
        return coriolis_peak * jnp.sin(math.pi * ((row.astype(F32) + offset) / ny - 0.5))

    for f, offset in enumerate((0.5, 1.0)):
        turning = coriolis(offset)
        for r in range(R):
            cor[f, r] = jnp.broadcast_to(turning[:, r : r + 1], (8, B))

    def prepare(cells, count, bend, beyond_fold, momentum, size=9):
        def get(f, i, r):
            if r == -1:
                return below(flow[f, i, count - 1])
            if r == count:
                return above(flow[f, i, 0])
            return flow[f, i, r]

        for start in range(0, len(cells), size):
            chunk = cells[start : start + size]

            def put(ref, index, x):
                for (i, r), y in zip(chunk, x.parts, strict=True):
                    held_back.append((ref, (index, i, r), y))

            def bent(a, b):
                return Batch(
                    jnp.where(beyond_fold, x, y) if r > bend else y
                    for (_, r), x, y in zip(chunk, a.parts, b.parts, strict=True)
                )

            held_back = []
            u0, v0 = (Batch(get(f, i, r) for i, r in chunk) for f in range(2))
            un, vn = (Batch(get(f, i, r + 1) for i, r in chunk) for f in range(2))
            w0 = Batch(wet[i, r] for i, r in chunk)
            wn = Batch(wet[i, r + 1] if r < count - 1 else above(wet[i, 0]) for i, r in chunk)
            gu = w0 * following(w0)
            gv = w0 * wn
            ue = following(u0)
            uw = preceding(u0)
            gw = preceding(gu)
            ua = bent(ue, u0)
            wa = bent(u0, uw)
            va = bent(vn, v0)
            put(cx, 0, gu)
            put(cx, 1, each(jnp.maximum, ua, 0.0) * gu)
            put(cx, 2, 0.5 - 0.5 * ua)
            put(cx, 3, gw)
            put(cx, 4, each(jnp.minimum, wa, 0.0) * gw)
            put(cx, 5, -0.5 - 0.5 * wa)
            put(cy, 0, gv)
            put(cy, 1, va * gv)
            put(cy, 2, where(va > 0.0, 0.5, -0.5) - 0.5 * va)
            for n, (i, r) in enumerate(chunk):
                if r == bend:
                    vf = jnp.where(beyond_fold, vn.parts[n], v0.parts[n])
                    held_back.append((fold, (0, i), vf * gv.parts[n]))
                    held_back.append((fold, (1, i), jnp.where(vf > 0.0, 0.5, -0.5) - 0.5 * vf))
            if momentum:
                us, vs = (Batch(get(f, i, r - 1) for i, r in chunk) for f in range(2))
                turn_u, turn_v = (Batch(cor[f, r] for _, r in chunk) for f in range(2))
                a = v0 + vs
                vbar = 0.25 * (a + following(a))
                a = u0 + un
                ubar = 0.25 * (a + preceding(a))
                du = vbar * (turn_u - 0.5 * (un - us)) - 0.5 * u0 * (ue - uw)
                dv = -ubar * (turn_v + 0.5 * (following(v0) - preceding(v0))) - 0.5 * v0 * (vn - vs)
                put(new, 0, u0 + gu * du)
                put(new, 1, v0 + gv * dv)
            flush(held_back)

    last = top & (sub == 7)
    last_strip = top & (sub >= 4)
    bend = R - H - 1

    def prepare_level(rows, i, carry):
        prepare([(i, r) for r in rows], R, bend, last, True)
        return carry

    lax.fori_loop(0, K, functools.partial(prepare_level, range(R)), 0)

    def face(w, c, here, there, slope_here, slope_there):
        way = w > 0.0
        return w * (jnp.where(way, here, there) + c * jnp.where(way, slope_here, slope_there))

    def advect(i, count, bend):
        first, held_back = [None] * T, []
        turned, last_jump, last_slope = [], [], []
        now, ahead, jump, slope, south = [], [], [], [], []
        for t in range(T):
            x0, x1 = tr[t, i, 0], tr[t, i, 1]
            xr = above(x0)
            jr = (xr - tr[t, i, count - 1]) * cy[0, i, count - 1]
            j0 = (x1 - x0) * cy[0, i, 0]
            s0 = minmod(j0, below(jr))
            turned.append(xr)
            last_jump.append(jr)
            last_slope.append(above(s0))
            now.append(x0)
            ahead.append(x1)
            jump.append(j0)
            slope.append(s0)
            south.append(None)
        state = {}

        def stage_a(t, r):
            x = tr[t, i, r]
            state[t, r] = (following(x), preceding(x))

        def stage_b(t, r):
            e, p = state[t, r]
            x = tr[t, i, r]
            s = minmod((e - x) * cx[0, i, r], (x - p) * cx[3, i, r])
            a = cx[1, i, r] * (x + cx[2, i, r] * s)
            b = cx[4, i, r] * (x + cx[5, i, r] * s)
            state[t, r] = (b - a, preceding(a), following(b))

        def stage_e(t, r):
            own, a, b = state.pop((t, r))
            x, xn = now[t], ahead[t]
            if r + 1 < count - 1:
                xnn = tr[t, i, r + 2]
                jn = (xnn - xn) * cy[0, i, r + 1]
                sn = minmod(jn, jump[t])
            elif r + 1 == count - 1:
                xnn = turned[t]
                jn = last_jump[t]
                sn = minmod(jn, jump[t])
            else:
                xnn = jn = None
                sn = last_slope[t]
            north = face(cy[1, i, r], cy[2, i, r], x, xn, slope[t], sn)
            y = x - north if r == 0 else x - (north - south[t])
            if r == bend:
                north = face(fold[0, i], fold[1, i], x, xn, slope[t], sn)
            south[t] = north
            now[t], ahead[t], jump[t], slope[t] = xn, xnn, jn, sn
            y = y + (own + (a - b))
            if r == 0:
                first[t] = y
            else:
                held_back.append((tr, (t, i, r), y))

        stages = [stage_a, stage_b, stage_e]
        for tick in range(count + 2 * DEPTH):
            for n in (2, 1, 0):
                r = tick - n * DEPTH
                if 0 <= r < count:
                    for t in range(T):
                        stages[n](t, r)
            if tick % 3 == 2:
                flush(held_back)
        flush(held_back)
        for t in range(T):
            tr[t, i, 0] = first[t] + below(south[t])

    def advect_level(i, carry):
        advect(lax.rem(i, K + 1), R, bend)
        return carry

    def advect_inner(i, carry):
        advect(lax.rem(i, K), R, bend)
        return carry

    lax.fori_loop(0, 2 * K, advect_inner, 0)

    for copy in sends:
        copy.wait_send()

    @pl.when(top)
    def _():
        for copy in over_fold:
            copy.wait_send()

    @pl.when(jnp.logical_not(top))
    def _():
        for copy in to_north:
            copy.wait_send()
        north_east.wait_send()
        north_west.wait_send()

    @pl.when(top & own_w)
    def _():
        self_west.wait()

    @pl.when(top & jnp.logical_not(own_w))
    def _():
        fold_west.wait_send()

    @pl.when(top & own_e)
    def _():
        self_east.wait()

    @pl.when(top & jnp.logical_not(own_e))
    def _():
        fold_east.wait_send()

    @pl.when(jnp.logical_not(bottom))
    def _():
        for copy in to_south:
            copy.wait_send()
        south_east.wait_send()
        south_west.wait_send()

    for copy in sends:
        copy.wait_recv()
    for copy in to_south:
        copy.wait_recv()

    @pl.when(jnp.logical_not(top & own_w))
    def _():
        south_east.wait_recv()

    @pl.when(jnp.logical_not(top & own_e))
    def _():
        south_west.wait_recv()

    @pl.when(jnp.logical_not(bottom))
    def _():
        for copy in to_north:
            copy.wait_recv()
        north_east.wait_recv()
        north_west.wait_recv()


    for f, n, at in ROWS:
        pending.append((ext, (f, lo), hs[pl.ds(at + n, 8)]))
        pending.append((ext, (f, beyond), hn[pl.ds(at + H, 8)]))
    flush(pending)

    @pl.when(bottom)
    def _():
        for f in range(WET, Q + T * K):
            ext[f, lo] = jnp.zeros((H, B), F32)
        pe[lo_land] = jnp.zeros((2 * H, B), F32)
        pw[lo_land] = jnp.zeros((2 * H, B), F32)

    @pl.when(top)
    def _():
        whole = B - 1 - lane
        turned = [flipped(hn[pl.ds(at + n, 8)], whole) for _, n, at in ROWS]
        for f, x in enumerate(turned, WET):
            ext[f, beyond] = -x if U <= f < Q else x
        within = 7 - lane % 8
        from_east = (lane // 8 + 15) % 16 * 8 + within
        from_west = (lane // 8 + 1) % 16 * 8 + within
        first, second = pl.ds(2 * H + B, H), pl.ds(3 * H + B, H)
        for landed, source in ((pe, from_east), (pw, from_west)):
            x, y = flipped(landed[first], source), flipped(landed[second], source)
            landed[first] = -y
            landed[second] = x

    def spread(n, parts, pack_e, pack_w, slot, own):
        x = where(far_hi, rolled(pack_e, 10 - 8 * slot), own)
        x = where(far_lo, rolled(pack_w, 22 - 8 * slot), x)
        for part, y in zip(parts, x.parts, strict=True):
            pending.append((pn, (n, part), y))

    corners = ((lo, beyond), (lo, pl.ds(3 * H + B, H)), (pl.ds(H, H), pl.ds(2 * H + B, H)))
    order = ((0, 3), (3, 0), (4, 1), (5, 2), (1, 0), (2, 1))
    landings = [corners[2] if n in (1, 2) else corners[1] for n, _ in order]
    far = [
        [rolled(Batch(pack[part] for part in landed), offset - 8 * slot) for landed, (_, slot) in zip(landings, order)]
        for pack, offset in ((pe, 10), (pw, 22))
    ]
    picks = [
        [picked(Batch(ext[FIELDS[n] + k, part] for part in corners[0]), source_of) for k in range(K)] for n, _ in order
    ]
    for (n, _), x, far_e, far_w in zip(order, picks, *far):
        edge = x[0]
        for k in range(1, K):
            edge = where(level == k, x[k], edge)
        edge = where(far_lo, far_w, where(far_hi, far_e, edge))
        for part, y in zip(corners[0], edge.parts, strict=True):
            pending.append((pn, (n, part), y))
    landed = [pl.ds(i * 8 + 2 * H, 8) for i in range(B // 8)]
    pack_e, pack_w = (Batch(pack[part] for part in landed) for pack in (pe, pw))
    for n, slot in ((0, 3), (3, 0), (4, 1), (5, 2)):
        spread(n, held_blocks, pack_e, pack_w, slot, read(pn, n))
    from_spare_e = jnp.where(place < 12, lane - 4, lane + 2)
    from_spare_w = jnp.where(place < 20, lane - 18, lane - 12)
    from_spare = jnp.where(place < 16, from_spare_e, from_spare_w) % B
    x = where(far_hi, picked(pack_e, from_spare), read(pn, 2))
    far_v = where(far_lo, picked(pack_w, from_spare), x)
    write(pn, (2,), far_v)
    flush(pending)
    run_hi = (place >= 9) & (place < 14)
    run_lo = (place >= 17) & (place < 23)
    own = read(pn, 1)
    dv = far_v - Batch(pn[2, pl.ds(i * 8 + H - 1, 8)] for i in range(B // 8))
    x = where(run_hi, where(place == 9, own, -dv), 0.0)
    y = where(run_lo, where(place == 22, own, rolled(dv, -1)), 0.0)
    x2, y2 = x + rolled(x, 1), y + rolled(y, -1)
    x, y = x2 + rolled(x2, 2) + rolled(x, 4), y2 + rolled(y2, -2) + rolled(y2, -4)
    write(pn, (1,), where(far_hi, x, where(far_lo, y, own)))
    flush(pending)
    for r in range(R):
        for n in range(len(FIELDS)):
            keep(n, K, r, pn[n, pl.ds(r, 8, stride=R)])
        flush(pending)

    flat = ext.reshape(32 * E, B)
    for r in range(S):
        for n, field in enumerate(FIELDS):
            south_rows = flat[pl.ds(field * E + H - 6 + r, 8, stride=E), :]
            north_rows = flat[pl.ds((field - K) * E + H + 120 + r, 8, stride=E), :]
            keep(n, K + 1, r, jnp.where(sub < 4, south_rows, north_rows))
        flush(pending)

    for r in (6, 7, 10, 11):
        for n in range(3):
            levels(n, r)
        flush(pending)
    prepare([(K, r) for r in range(R)], R, bend, last, True, R)
    prepare([(K + 1, r) for r in range(S)], S, 7, last_strip, False, S)
    prepare([(k, r) for k in range(K) for r in range(6, 11)], R, bend, last, True, 20)

    def advect_edges(i, carry):
        advect(K, R, bend)
        advect(K + 1, S, 7)
        return carry

    lax.fori_loop(0, 2, advect_edges, 0, unroll=True)

    ends = (sub == 0) | (sub == 7)
    for t in range(T):
        strip = [
            jnp.take_along_axis(tr[t, K + 1, r - 2], jnp.where(sub == 0, k, 4 + k), axis=0)
            for k in range(K)
            for r in range(6, 12)
        ]
        edge = Batch(tr[t, K, r] for r in range(R))
        x = [
            [jnp.where(ends, strip[6 * k + r - 6], tr[t, k, r]) if 6 <= r < 12 else tr[t, k, r] for r in range(R)]
            for k in range(K)
        ]
        x = [merged(Batch(x[k]), edge, k, 4, B - 4) for k in range(K)]
        for k in range(K):
            for r in range(R):
                pending.append((tr, (t, k, r), x[k].parts[r]))
        flush(pending)

    lax.fori_loop(0, K + 1, advect_level, 0, unroll=True)

    for start in range(0, R, 6):
        strided = [pl.ds(r, 8, stride=R) for r in range(start, start + 6)]

        def rows_of(ref, *index):
            return Batch(ref[(*index, r)] for r in range(start, start + 6))

        def both(ref, first, k, low, high):
            return merged(rows_of(ref, *first, k), rows_of(ref, *first, K), k, low, high)

        def leave(first, solved):
            for k in range(K):
                for part, x in zip(strided, solved[k].parts, strict=True):
                    pending.append((res, (first + k, part), x))

        mix = [Batch(dext[k, part] for part in strided) for k in range(K - 1)]
        gu = [both(cx, (0,), k, 0, B - 1) for k in range(K)]
        un = [both(new, (0,), k, 1, B - 1) for k in range(K)]
        coupling = [mix[k] * (gu[k] * gu[k + 1]) for k in range(K - 1)]
        un = solve(un, coupling, *factored(coupling))
        leave(0, un)
        gv = [rows_of(cy, 0, k) for k in range(K)]
        vn = [both(new, (1,), k, 1, B - 1) for k in range(K)]
        coupling = [mix[k] * (gv[k] * gv[k + 1]) for k in range(K - 1)]
        vn = solve(vn, coupling, *factored(coupling))
        leave(K, vn)
        flush(pending)


def stepped(nlat, nlon, u, v, q, m, d):
    hbm = pl.BlockSpec(memory_space=pltpu.HBM)
    return pl.pallas_call(
        functools.partial(step, nlat, nlon),
        out_shape=[
            jax.ShapeDtypeStruct((2 * K, E, B), F32),
            jax.ShapeDtypeStruct((T, K + 2, R, 8, B), F32),
            jax.ShapeDtypeStruct((K + 2, R, 8, B), F32),
            jax.ShapeDtypeStruct((K - 1, E, B), F32),
        ],
        in_specs=[hbm] * 5,
        out_specs=[pl.BlockSpec(memory_space=pltpu.VMEM)] * 4,
        scratch_shapes=[
            pltpu.VMEM((32, E, B), F32),
            pltpu.VMEM((K, B, B), jnp.int32),
            pltpu.VMEM((SENT + 2 * H, B), F32),
            pltpu.VMEM((SENT + 2 * H, B), F32),
            pltpu.VMEM((B + 4 * H, B), F32),
            pltpu.VMEM((B + 4 * H, B), F32),
            pltpu.VMEM((SENT + H, B), F32),
            pltpu.VMEM((SENT + H, B), F32),
            pltpu.VMEM((E, B), F32),
            pltpu.VMEM((E, B), F32),
            pltpu.VMEM((len(FIELDS), E, B), F32),
            pltpu.VMEM((2, K + 2, R, 8, B), F32),
            pltpu.VMEM((2, K + 1, R, 8, B), F32),
            pltpu.VMEM((6, K + 2, R, 8, B), F32),
            pltpu.VMEM((3, K + 2, R, 8, B), F32),
            pltpu.VMEM((2, K + 2, 8, B), F32),
            pltpu.VMEM((2, R, 8, B), F32),
            pltpu.SemaphoreType.DMA((15,)),
            pltpu.SemaphoreType.DMA((8,)),
            pltpu.SemaphoreType.DMA((8,)),
        ],
        compiler_params=pltpu.CompilerParams(
            collective_id=0, has_side_effects=True, vmem_limit_bytes=40 * 2**20
        ),
    )(u, v, q, m, d)


def deliver(res, tr, wet, dext, u, v, q, out, done):
    middle = pl.ds(H, B)
    copies = [
        pltpu.make_async_copy(res.at[0:K, middle], u, done.at[0]),
        pltpu.make_async_copy(res.at[K : 2 * K, middle], v, done.at[1]),
    ]
    for copy in copies:
        copy.start()
    factors = []
    for start in range(0, R, 6):
        rows = range(start, start + 6)
        w = [Batch(wet[k, r] for r in rows) for k in range(K)]
        mix = [Batch(dext[k, pl.ds(r, 8, stride=R)] for r in rows) for k in range(K - 1)]
        coupling = [mix[k] * (w[k] * w[k + 1]) for k in range(K - 1)]
        factors.append((rows, coupling, *factored(coupling)))
    for t in range(T):
        for rows, *factor in factors:
            edge = Batch(tr[t, K, r] for r in rows)
            x = [merged(Batch(tr[t, k, r] for r in rows), edge, k, 2, B - 2) for k in range(K)]
            for k, solved in enumerate(solve(x, *factor)):
                for r, y in zip(rows, solved.parts, strict=True):
                    out[t * K + k, pl.ds(r, 8, stride=R)] = y
        part = pl.ds(t * K, K)
        copies.append(pltpu.make_async_copy(out.at[part, middle], q.at[part], done.at[2 + t]))
        copies[-1].start()
    for copy in copies:
        copy.wait()


def delivered(given):
    return pl.pallas_call(
        deliver,
        out_shape=(
            jax.ShapeDtypeStruct((K, B, B), F32),
            jax.ShapeDtypeStruct((K, B, B), F32),
            jax.ShapeDtypeStruct((T * K, B, B), F32),
        ),
        in_specs=[pl.BlockSpec(memory_space=pltpu.VMEM)] * 4,
        out_specs=[pl.BlockSpec(memory_space=pltpu.HBM)] * 3,
        scratch_shapes=[pltpu.VMEM((T * K, E, B), F32), pltpu.SemaphoreType.DMA((2 + T,))],
    )(*given)


def per_device(nlat, nlon, zonal_flow, meridional_flow, tracers, sea_mask, diffusivity):
    q = tracers.reshape(T * K, B, B)
    given = [
        pltpu.with_memory_space_constraint(x, pltpu.HBM)
        for x in (zonal_flow, meridional_flow, q, sea_mask, diffusivity)
    ]
    kept = [pltpu.with_memory_space_constraint(x, pltpu.VMEM) for x in stepped(nlat, nlon, *given)]
    u, v, q = delivered(kept)
    return u, v, q.reshape(T, K, B, B)


def solution(mesh):
    cells = P(None, "lat", "lon")
    traced = P(None, None, "lat", "lon")
    return jax.shard_map(
        functools.partial(per_device, mesh.shape["lat"], mesh.shape["lon"]),
        mesh=mesh,
        in_specs=(cells, cells, traced, cells, cells),
        out_specs=(cells, cells, traced),
        check_vma=False,
    )
```
